256 devices in a mesh: row: 32 (over x_hi, z, core), col: 8 (over y, x_lo).
Axes of the slice: x: 4 (x_hi: 2, x_lo: 2; x = x_hi * 2 + x_lo), y: 4, z: 8, core: 2. Of those that a mesh axis runs over, the one named last changes fastest.
Arguments:
- features: bfloat16 [65536, 256], P(('row', 'col')), may hold values from -6 to 6
- degrees: int32 [65536], P(('row', 'col')), may hold values from 1 to 64
- blocks: bfloat16 [1024, 88, 128, 128], P('row', 'col'), may hold values from 0 to 2
- block_ids: int32 [1024, 88], P('row', 'col'), may hold values from 0 to 31, as said below
- counts: int32 [1024, 8], P('row', 'col'), may hold values from 1 to 11, as said below
- weight: bfloat16 [256, 256], replicated, may hold values from -0.375 to 0.375
- out_bias: float32 [256], replicated, may hold values from -3 to 3
Outputs:
- mixed: bfloat16 [65536, 256], P(('row', 'col'))
The draws below stay inside these ranges and needn't reach their ends.
Inputs may be any that keep to these rules, and one draw needn't show every extreme that they name: `block_ids`: within each list of 11 slots (live or not) the codes are distinct. `counts`: every tile has one segment whose list is full.
All inputs are finite; a program needn't handle non-finite values.
Results may differ from the reference program's by a relative error of at most 0.018.
Values may be sent and summed in bfloat16 or wider, within the bound.
A program may use at most 128 MiB of HBM per device.

```python
import jax
import jax.numpy as jnp
from jax import lax

FEAT = 256
BS = 128
ROWS_DEV = 256
GRIDROWS = 32
GRIDCOLS = 8
SUBTOTAL = 1024
MAXS = 11
NODES = 65536


def draw_blocks(key, part):
    shape = (SUBTOTAL, GRIDCOLS * MAXS, BS, BS)
    logs = jax.random.uniform(jax.random.fold_in(key, 31), shape, jnp.float32, jnp.log(0.1), jnp.log(2.0))
    present = jax.random.uniform(jax.random.fold_in(key, 32), shape, jnp.float32) < 0.25
    return jnp.where(present, jnp.exp(logs), 0.0).astype(jnp.bfloat16)


def draw_block_ids(key, part):
    per_segment = ROWS_DEV // BS * (ROWS_DEV * GRIDCOLS // BS)
    keys = jax.random.split(jax.random.fold_in(key, 11), SUBTOTAL * GRIDCOLS)

    def single(single_key):
        return jax.random.permutation(single_key, per_segment)[:MAXS]
    chosen = jax.vmap(single)(keys)
    return chosen.reshape(SUBTOTAL, GRIDCOLS * MAXS).astype(jnp.int32)


def draw_counts(key, part):
    uniform_part = jax.random.randint(jax.random.fold_in(key, 21), (GRIDROWS, GRIDROWS, GRIDCOLS), 0, MAXS)
    factor = jax.random.randint(jax.random.fold_in(key, 22), (GRIDROWS, 1, GRIDCOLS), 1, 5)
    filled = 1 + uniform_part * factor // 4
    full_at = jax.random.randint(jax.random.fold_in(key, 23), (GRIDROWS, 1, GRIDCOLS), 0, GRIDROWS)
    filled = jnp.where(jnp.arange(GRIDROWS)[None, :, None] == full_at, MAXS, filled)
    return filled.reshape(SUBTOTAL, GRIDCOLS).astype(jnp.int32)


def set_ends(values, own_key, low, largest):
    longest = values.shape.index(max(values.shape))
    spots = []
    for shift in (0, 1):
        where = [jax.random.randint(jax.random.fold_in(own_key, axis), (), 0, length) for axis, length in enumerate(values.shape)]
        where[longest] = (where[longest] + shift) % values.shape[longest]
        spots.append(tuple(where))
    return values.at[spots[0]].set(low).at[spots[1]].set(largest)


def shard_levels(key, dims, shards, least, top_value):
    level, own = 1.0, jax.random.fold_in(key, 6)
    for position, blocks in shards:
        heights = jnp.exp(jax.random.uniform(jax.random.fold_in(own, position), (blocks,), jnp.float32, least / len(shards), top_value / len(shards)))
        level = level * jnp.repeat(heights, dims[position] // blocks).reshape([-1 if axis == position else 1 for axis in range(len(dims))])
    return level


def scatter_about(key, shape, scale, most, cuts=(), held_as=jnp.bfloat16):
    factor_of = shard_levels(key, shape, cuts, -0.22, 0.18) if cuts else 1.0
    values = jax.random.normal(key, shape, jnp.float32) * scale * factor_of
    return jnp.minimum(jnp.maximum(values, -most), most).astype(held_as)


def setup_inputs(seed: int = 0) -> dict:
    splits = jax.random.split(jax.random.key(seed), 8)
    features = scatter_about(splits[0], (NODES, FEAT), 1.0, 6.0, ((0, 256),))
    degrees = set_ends(jax.random.randint(splits[1], (NODES,), 1, 65), jax.random.fold_in(splits[1], 1), 1, 64).astype(jnp.int32)
    blocks = draw_blocks(jax.random.fold_in(splits[7], 71), 0)
    block_ids = draw_block_ids(jax.random.fold_in(splits[7], 71), 0)
    counts = draw_counts(jax.random.fold_in(splits[7], 71), 0)
    weight = scatter_about(splits[5], (FEAT, FEAT), FEAT ** -0.5, 0.375)
    out_bias = scatter_about(splits[6], (FEAT,), 0.5, 3.0, (), jnp.float32)
    return dict(features=features, degrees=degrees, blocks=blocks, block_ids=block_ids, counts=counts, weight=weight, out_bias=out_bias)


def slot_term(block_vals, slot_codes, live_count, gathered):
    col_blocks = gathered.shape[0] // BS
    row_blocks = ROWS_DEV // BS
    col_place = slot_codes % col_blocks
    row_place = slot_codes // col_blocks
    pieces = jnp.take(gathered.reshape(col_blocks, BS, FEAT), col_place, axis=0)
    products = jnp.einsum('kij,kjf->kif', block_vals.astype(jnp.float32), pieces.astype(jnp.float32), precision=lax.Precision.HIGHEST)
    occupied = jnp.arange(slot_codes.shape[0]).astype(jnp.int32) < live_count
    select = ((row_place[:, None] == jnp.arange(row_blocks).astype(jnp.int32)[None, :]) & occupied[:, None]).astype(jnp.float32)
    summed = jnp.einsum('kr,kif->rif', select, products, precision=lax.Precision.HIGHEST)
    return summed.reshape(ROWS_DEV, FEAT)

def reference(features, degrees, blocks, block_ids, counts, weight, out_bias):
    scaling = lax.rsqrt(degrees.astype(jnp.float32))[:, None]
    scaled = (features.astype(jnp.float32) * scaling).astype(jnp.bfloat16)
    group_rows = ROWS_DEV * GRIDCOLS
    shaped_blocks = blocks.reshape(SUBTOTAL, GRIDCOLS, MAXS, BS, BS)
    shaped_codes = block_ids.reshape(SUBTOTAL, GRIDCOLS, MAXS)

    def visit(pair_index, totals):
        pair_index = jnp.asarray(pair_index).astype(jnp.int32)
        entry_row = pair_index // GRIDCOLS
        column = pair_index % GRIDCOLS
        grid_row = entry_row // GRIDROWS
        subrange = entry_row % GRIDROWS
        gathered = lax.dynamic_slice_in_dim(scaled, (grid_row * group_rows).astype(jnp.int32), group_rows, 0)
        contrib = slot_term(shaped_blocks[entry_row, column], shaped_codes[entry_row, column], counts[entry_row, column], gathered)
        contrib = lax.optimization_barrier(contrib.astype(jnp.bfloat16)).astype(jnp.float32)
        offset = ((subrange * GRIDCOLS + column) * ROWS_DEV).astype(jnp.int32)
        current = lax.dynamic_slice_in_dim(totals, offset, ROWS_DEV, 0)
        return lax.dynamic_update_slice_in_dim(totals, current + contrib, offset, 0)
    summed = lax.fori_loop(0, SUBTOTAL * GRIDCOLS, visit, jnp.zeros((NODES, FEAT), jnp.float32))
    combined = (scaling * (summed + scaled.astype(jnp.float32))).astype(jnp.bfloat16)
    mixed = jnp.dot(combined, weight, preferred_element_type=jnp.float32) + out_bias.astype(jnp.float32)
    return jnp.maximum(mixed, 0.0).astype(jnp.bfloat16)
```

```python
import functools

import jax
import jax.numpy as jnp
from jax import lax
from jax.experimental import pallas as pl
from jax.experimental.pallas import tpu as pltpu
from jax.sharding import PartitionSpec as P

MESH = pl.DeviceIdType.MESH
BF = jnp.bfloat16
F32 = jnp.float32
NZ = 8
NY = 4
SEGS = 32
SLOTS = 11
BS = 128
ROWS = 256
FEAT = 256
WAVE = [0, 0, 0, 1, 0, 0, 1, 1, 0, 0, 1, 1, 0, 1, 1, 1]
DIST = [4, 3, -3, 4, 2, -2, 3, -3, 1, -1, 2, -2, 0, 1, -1, 0]
TASK = {(w, d): i for i, (w, d) in enumerate(zip(WAVE, DIST))}


def pick(table, index):
    value = jnp.int32(table[0])
    for i in range(1, len(table)):
        value = jnp.where(index >= i, jnp.int32(table[i]), value)
    return value


def kernel(
    deg_ref, feat_ref, blocks_ref, ids_ref, cnt_ref, weight_ref, bias_ref, out_ref,
    gat, stage, left, own, sib_out, sib_in, z_out, z_in, z_in2, x_out, x_in, scal,
    stage_sem, ag_send, ag_recv, sib_send, sib_recv, z_send, z_recv, z_send2, z_recv2, x_send, x_recv,
):
    row, col = lax.axis_index("row"), lax.axis_index("col")
    core = row % 2
    z = (row // 2) % NZ
    xh = row // (2 * NZ)
    y, xl = col // 2, col % 2

    def at(xh_, z_, core_):
        return xh_ * (2 * NZ) + z_ * 2 + core_

    z_up = (at(xh, (z + 1) % NZ, core), col)
    z_dn = (at(xh, (z + NZ - 1) % NZ, core), col)
    sib = (at(xh, z, 1 - core), col)
    x_far = (at(1 - xh, z, core), col)
    c_up = ((y + 1) % NY) * 2 + xl
    c_dn = ((y + NY - 1) % NY) * 2 + xl
    c_x = y * 2 + 1 - xl
    c_two = ((y + 2) % NY) * 2 + xl
    y_up, y_dn, x_near = (row, c_up), (row, c_dn), (row, c_x)
    cx_up = ((y + 1) % NY) * 2 + 1 - xl
    cx_dn = ((y + NY - 1) % NY) * 2 + 1 - xl
    cx_two = ((y + 2) % NY) * 2 + 1 - xl

    barrier = pltpu.get_barrier_semaphore()
    for other in (z_up, z_dn, sib, x_far, y_up, y_dn, x_near):
        pl.semaphore_signal(barrier, inc=1, device_id=other, device_id_type=MESH)

    loads = [
        pltpu.make_async_copy(
            blocks_ref.at[pl.ds(4 * i, 4)], stage.at[pl.ds(4 * i, 4)], stage_sem.at[i]
        )
        for i in range(8)
    ]
    for load in loads:
        load.start()

    rows = lax.broadcasted_iota(jnp.int32, (ROWS, ROWS), 0)
    cols = lax.broadcasted_iota(jnp.int32, (ROWS, ROWS), 1)
    degs = jnp.broadcast_to(deg_ref[...].astype(F32), (ROWS, ROWS))
    scaling = lax.rsqrt(jnp.sum(jnp.where(rows == cols, degs, 0.0), axis=1, keepdims=True))
    scal[...] = scaling
    scaled = (feat_ref[...].astype(F32) * scaling).astype(BF)
    gat[2 * col] = scaled[:BS]
    gat[2 * col + 1] = scaled[BS:]

    pl.semaphore_wait(barrier, 7)

    def ag(source, half, send, recv, target):
        block = gat.at[2 * source + half]
        return pltpu.make_async_remote_copy(
            src_ref=block, dst_ref=block, send_sem=ag_send.at[send], recv_sem=ag_recv.at[recv],
            device_id=target, device_id_type=MESH,
        )

    def landed(source, half, recv):
        ag(source, half, 0, recv, y_up).wait_recv()

    sends = []
    for half in (0, 1):
        sends += [
            ag(col, half, half, half, y_up),
            ag(col, half, 2 + half, 2 + half, y_dn),
            ag(col, half, 4 + half, 4 + half, x_near),
        ]
    for copy in sends:
        copy.start()

    def prepare(first, last):
        for i in range(first // 4, last // 4):
            loads[i].wait()

        def body(s, carry):
            live = cnt_ref[s, 0]
            for k in range(SLOTS):
                q = ids_ref[s, k]
                block = stage[s, k]
                top = jnp.where((q < 16) & (k < live), 1.0, 0.0).astype(F32)
                low = jnp.where((q >= 16) & (k < live), 1.0, 0.0).astype(F32)
                left[s, :BS, k * BS:(k + 1) * BS] = block * jnp.full((BS, BS), top, F32).astype(BF)
                left[s, BS:, k * BS:(k + 1) * BS] = block * jnp.full((BS, BS), low, F32).astype(BF)
            return carry

        lax.fori_loop(first, last, body, 0)

    prepare(0, 12)

    def relay(source, half, recv, *copies):
        landed(source, half, recv)
        for copy in copies:
            copy.start()
            sends.append(copy)

    relay(c_dn, 0, 0, ag(c_dn, 0, 6, 6, y_up))
    relay(c_x, 0, 4, ag(c_x, 0, 8, 8, y_up), ag(c_x, 0, 10, 10, y_dn))
    relay(c_up, 1, 3, ag(c_up, 1, 7, 7, y_dn))
    relay(c_x, 1, 5, ag(c_x, 1, 9, 9, y_up), ag(c_x, 1, 11, 11, y_dn))
    prepare(12, 24)
    relay(c_two, 0, 6, ag(c_two, 0, 12, 12, x_near))
    relay(c_two, 1, 7, ag(c_two, 1, 13, 13, x_near))
    prepare(24, 32)
    landed(c_dn, 1, 1)
    landed(c_up, 0, 2)
    for half in (0, 1):
        landed(cx_dn, half, 8 + half)
        landed(cx_up, half, 10 + half)
        landed(cx_two, half, 12 + half)

    def term(s):
        right = jnp.concatenate([gat[ids_ref[s, k] % 16] for k in range(SLOTS)], axis=0)
        return jnp.dot(left[s], right, preferred_element_type=F32)

    def sib_copy(i):
        return pltpu.make_async_remote_copy(
            src_ref=sib_out.at[i], dst_ref=sib_in.at[i], send_sem=sib_send.at[i], recv_sem=sib_recv.at[i],
            device_id=sib, device_id_type=MESH,
        )

    def z_copy(task, half=None):
        w, d = WAVE[task], DIST[task]
        if d == 4:
            then, target = (TASK[w, 3], z_up) if half == 0 else (TASK[w, -3], z_dn)
            part = pl.ds(half * BS, BS)
            second = half == 1
            return pltpu.make_async_remote_copy(
                src_ref=z_out.at[task, part], dst_ref=z_in.at[then, part],
                send_sem=(z_send2 if second else z_send).at[w if second else task], recv_sem=z_recv.at[then],
                device_id=target, device_id_type=MESH,
            )
        then, target = (TASK[w, d - 1], z_up) if d > 0 else (TASK[w, d + 1], z_dn)
        if d == -1:
            dst, recv = z_in2.at[w], z_recv2.at[w]
        else:
            dst, recv = z_in.at[then], z_recv.at[then]
        return pltpu.make_async_remote_copy(
            src_ref=z_out.at[task], dst_ref=dst, send_sem=z_send.at[task], recv_sem=recv,
            device_id=target, device_id_type=MESH,
        )

    x_copy = pltpu.make_async_remote_copy(
        src_ref=x_out, dst_ref=x_in, send_sem=x_send, recv_sem=x_recv, device_id=x_far, device_id_type=MESH
    )

    def finish(i):
        w, d = WAVE[i], DIST[i]
        sib_copy(i).wait_recv()
        if d == 3:
            z_copy(TASK[w, 4], 0).wait_recv()
        elif d == -3:
            z_copy(TASK[w, 4], 1).wait_recv()
        elif d > 0 and d < 3:
            z_copy(TASK[w, d + 1]).wait_recv()
        elif d < 0:
            z_copy(TASK[w, d - 1]).wait_recv()
        elif d == 0:
            z_copy(TASK[w, 1]).wait_recv()
            z_copy(TASK[w, -1]).wait_recv()
        if i == 15:
            return
        dest = x_out if d == 0 else z_out.at[i]
        for half in (0, 1):
            part = pl.ds(half * BS, BS)
            value = own[i, part] + sib_in[i, part].astype(F32)
            if d in (1, 2, -1, -2, 0) or (d == 3 and half == 0) or (d == -3 and half == 1):
                value = value + z_in[i, part].astype(F32)
            if d == 0:
                value = value + z_in2[w, part].astype(F32)
            dest[part] = value.astype(BF)
        if d == 4:
            z_copy(i, 0).start()
            z_copy(i, 1).start()
        elif d == 0:
            x_copy.start()
        else:
            z_copy(i).start()

    def step(i, carry):
        @pl.when(i < 16)
        def _():
            w, d = pick(WAVE, i), pick(DIST, i)
            target_x = w * xh + (1 - w) * (1 - xh)
            target_z = (z + d + NZ) % NZ
            sib_out[i] = term(at(target_x, target_z, 1 - core)).astype(BF)
            sib_copy(i).start()
            own[i] = term(at(target_x, target_z, core))

        for k in range(16):
            pl.when(i == k + 1)(functools.partial(finish, k))
        return carry

    lax.fori_loop(0, 17, step, 0)

    x_copy.wait_recv()
    summed = (
        own[15] + sib_in[15].astype(F32) + z_in[15].astype(F32) + z_in2[1].astype(F32) + x_in[...].astype(F32)
    )
    own_rows = jnp.concatenate([gat[2 * col], gat[2 * col + 1]], axis=0).astype(F32)
    combined = (scal[...] * (summed + own_rows)).astype(BF)
    mixed = jnp.dot(combined, weight_ref[...], preferred_element_type=F32) + bias_ref[...]
    out_ref[...] = jnp.maximum(mixed, 0.0).astype(BF)

    for copy in sends:
        copy.wait_send()
    for i in range(16):
        sib_copy(i).wait_send()
        if DIST[i] == 4:
            z_copy(i, 0).wait_send()
            z_copy(i, 1).wait_send()
        elif DIST[i] != 0:
            z_copy(i).wait_send()
    x_copy.wait_send()


def local(features, degrees, blocks, block_ids, counts, weight, out_bias):
    vmem = pl.BlockSpec(memory_space=pltpu.VMEM)
    smem = pl.BlockSpec(memory_space=pltpu.SMEM)
    full = (ROWS, FEAT)
    dma = pltpu.SemaphoreType.DMA
    return pl.pallas_call(
        kernel,
        out_shape=jax.ShapeDtypeStruct(full, BF),
        in_specs=[vmem, vmem, pl.BlockSpec(memory_space=pl.ANY), smem, smem, vmem, vmem],
        out_specs=vmem,
        scratch_shapes=[
            pltpu.VMEM((16, BS, FEAT), BF),
            pltpu.VMEM((SEGS, SLOTS, BS, BS), BF),
            pltpu.VMEM((SEGS, ROWS, SLOTS * BS), BF),
            pltpu.VMEM((16,) + full, F32),
            pltpu.VMEM((16,) + full, BF),
            pltpu.VMEM((16,) + full, BF),
            pltpu.VMEM((16,) + full, BF),
            pltpu.VMEM((16,) + full, BF),
            pltpu.VMEM((2,) + full, BF),
            pltpu.VMEM(full, BF),
            pltpu.VMEM(full, BF),
            pltpu.VMEM((ROWS, 1), F32),
            dma((8,)), dma((14,)), dma((14,)), dma((16,)), dma((16,)), dma((16,)), dma((16,)), dma((2,)), dma((2,)),
            dma, dma,
        ],
        compiler_params=pltpu.CompilerParams(
            collective_id=0, has_side_effects=True, vmem_limit_bytes=60 * 1024 * 1024
        ),
        cost_estimate=pl.CostEstimate(
            flops=2 * SEGS * ROWS * SLOTS * BS * FEAT, bytes_accessed=SEGS * SLOTS * BS * BS * 2, transcendentals=0
        ),
    )(degrees.reshape(1, ROWS), features, blocks, block_ids, counts, weight, out_bias.reshape(1, FEAT))


def solution(mesh):
    placed = (
        P(("row", "col"), None),
        P(("row", "col")),
        P("row", "col", None, None),
        P("row", "col"),
        P("row", "col"),
        P(),
        P(),
    )
    return jax.shard_map(
        local, mesh=mesh, in_specs=placed, out_specs=P(("row", "col"), None), check_vma=False
    )
```

```python
import functools

import jax
import jax.numpy as jnp
from jax import lax
from jax.experimental import pallas as pl
from jax.experimental.pallas import tpu as pltpu
from jax.sharding import PartitionSpec as P

MESH = pl.DeviceIdType.MESH
BF = jnp.bfloat16
F32 = jnp.float32
NZ = 8
NY = 4
SEGS = 32
SLOTS = 11
BS = 128
ROWS = 256
FEAT = 256
PIECES = 4
PIECE = ROWS // PIECES
X_FIRST = (0, 1)
HALF = [0, 1, 0, 0, 1, 1, 0, 0, 1, 1, 0, 0, 1, 1, 0, 1]
DIST = [4, 4, 3, -3, -3, 3, 2, -2, -2, 2, -1, 1, 1, -1, 0, 0]
TASK = {pair: i for i, pair in enumerate(zip(HALF, DIST))}
XSLOT = {d: i for i, d in enumerate((4, 3, -3, 2, -2, 1, -1, 0))}
FOLLOW = {
    3: [(0, 4, 1), (0, 4, 0), (0, 4, 3), (0, 4, 2)],
    4: [(1, 4, 3), (0, 3, 1), (0, 3, 0), (1, 4, 2), (0, 3, 3)],
    5: [(0, -3, 1), (0, -3, 0), (0, -3, 2)],
    6: [(1, 4, 1), (0, -3, 3), (0, 3, 2), (1, -3, 2), (1, 4, 0)],
    7: [(1, 3, 3), (1, 3, 2), (1, 3, 1), (1, -3, 3)],
    9: [(0, 2, 1), (0, 2, 0), (1, -3, 1), (1, -3, 0), (0, 2, 3), (0, -2, 1), (0, -2, 0), (0, 2, 2), (0, -2, 3),
        (1, 3, 0), (0, -2, 2)],
    10: [(1, -2, 2)],
    11: [(1, -2, 3)],
    12: [(1, 2, 3), (1, 2, 2), (1, 2, 1)],
    13: [(0, -1, 1), (0, -1, 0), (0, 1, 1), (0, 1, 0), (1, -2, 1), (0, 1, 3), (0, 1, 2), (1, -2, 0), (1, 2, 0),
         (0, -1, 3), (0, -1, 2)],
    15: [(1, 1, 3)],
    16: [(1, 1, 2), (1, -1, 3), (1, -1, 2), (1, -1, 1), (0, 0, 1), (0, 0, 0), (1, -1, 0), (1, 1, 1), (0, 0, 3),
         (1, 1, 0), (0, 0, 2), (1, 0, 1), (1, 0, 3), (1, 0, 0), (1, 0, 2)],
}


def pick(table, index):
    value = jnp.int32(table[0])
    for i in range(1, len(table)):
        value = jnp.where(index >= i, jnp.int32(table[i]), value)
    return value


def kernel(
    deg_hbm, feat_hbm, blocks_ref, ids_hbm, cnt_hbm, weight_hbm, bias_hbm, out_ref,
    deg_ref, feat_ref, ids_ref, cnt_ref, weight_ref, bias_ref,
    gat, stage, left, own, sib_out, sib_in, z_out, z_in, z_in2, x_in, scal,
    in_sem, stage_sem, ag_send, ag_recv, sib_send, sib_recv, z_send, z_recv, z_recv2, x_send, x_recv,
):
    row, col = lax.axis_index("row"), lax.axis_index("col")
    core = row % 2
    z = (row // 2) % NZ
    xh = row // (2 * NZ)
    y, xl = col // 2, col % 2

    def at(xh_, z_, core_):
        return xh_ * (2 * NZ) + z_ * 2 + core_

    z_up = (at(xh, (z + 1) % NZ, core), col)
    z_dn = (at(xh, (z + NZ - 1) % NZ, core), col)
    sib = (at(xh, z, 1 - core), col)
    x_far = (at(1 - xh, z, core), col)
    c_up = ((y + 1) % NY) * 2 + xl
    c_dn = ((y + NY - 1) % NY) * 2 + xl
    c_x = y * 2 + 1 - xl
    c_two = ((y + 2) % NY) * 2 + xl
    y_up, y_dn, x_near = (row, c_up), (row, c_dn), (row, c_x)

    barrier = pltpu.get_barrier_semaphore()
    for other in (z_up, z_dn, sib, x_far, y_up, y_dn, x_near):
        pl.semaphore_signal(barrier, inc=1, device_id=other, device_id_type=MESH)

    inputs = [
        pltpu.make_async_copy(src, dst, in_sem.at[i])
        for i, (src, dst) in enumerate((
            (deg_hbm, deg_ref), (feat_hbm, feat_ref), (ids_hbm, ids_ref), (cnt_hbm, cnt_ref),
            (weight_hbm, weight_ref), (bias_hbm, bias_ref),
        ))
    ]
    for copy in inputs:
        copy.start()
    loads = [
        pltpu.make_async_copy(
            blocks_ref.at[pl.ds(4 * i, 4)], stage.at[pl.ds(4 * i, 4)], stage_sem.at[i]
        )
        for i in range(8)
    ]
    for load in loads:
        load.start()
    inputs[0].wait()
    inputs[1].wait()

    rows = lax.broadcasted_iota(jnp.int32, (ROWS, ROWS), 0)
    cols = lax.broadcasted_iota(jnp.int32, (ROWS, ROWS), 1)
    degs = jnp.broadcast_to(deg_ref[...].astype(F32), (ROWS, ROWS))
    scaling = lax.rsqrt(jnp.sum(jnp.where(rows == cols, degs, 0.0), axis=1, keepdims=True))
    scal[...] = scaling
    scaled = (feat_ref[...].astype(F32) * scaling).astype(BF)
    gat[2 * col] = scaled[:BS]
    gat[2 * col + 1] = scaled[BS:]

    pl.semaphore_wait(barrier, 7)

    def piece_of(source, p):
        return gat.at[2 * source + p // 2, pl.ds((p % 2) * PIECE, PIECE)]

    def ag(source, p, send, recv, target):
        return pltpu.make_async_remote_copy(
            src_ref=piece_of(source, p), dst_ref=piece_of(source, p),
            send_sem=ag_send.at[send, p], recv_sem=ag_recv.at[recv, p],
            device_id=target, device_id_type=MESH,
        )

    FROM_DN, FROM_UP, FROM_X, TWO, X_DN, X_UP, X_TWO = range(7)
    source_of = {
        FROM_DN: c_dn, FROM_UP: c_up, FROM_X: c_x, TWO: c_two,
        X_DN: ((y + NY - 1) % NY) * 2 + 1 - xl, X_UP: ((y + 1) % NY) * 2 + 1 - xl, X_TWO: ((y + 2) % NY) * 2 + 1 - xl,
    }
    sends = []

    def send(*copies):
        for copy in copies:
            copy.start()
            sends.append(copy)

    def landed(kind, p):
        ag(source_of[kind], p, 0, kind, y_up).wait_recv()

    for a, b, c in zip((0, 2, 1, 3), (1, 3, 0, 2), (0, 1, 2, 3)):
        send(ag(col, a, 0, FROM_DN, y_up), ag(col, c, 2, FROM_X, x_near), ag(col, b, 1, FROM_UP, y_dn))

    def prepare(first, last):
        for i in range(first // 4, last // 4):
            loads[i].wait()

        def body(s, carry):
            live = cnt_ref[0, s]
            for k in range(SLOTS):
                q = ids_ref[k, s]
                block = stage[s, k]
                top = jnp.where((q < 16) & (k < live), 1.0, 0.0).astype(F32)
                low = jnp.where((q >= 16) & (k < live), 1.0, 0.0).astype(F32)
                left[s, :BS, k * BS:(k + 1) * BS] = block * jnp.full((BS, BS), top, F32).astype(BF)
                left[s, BS:, k * BS:(k + 1) * BS] = block * jnp.full((BS, BS), low, F32).astype(BF)
            return carry

        lax.fori_loop(first, last, body, 0)

    def relay_x(p):
        landed(FROM_X, p)
        send(ag(c_x, p, 3, X_DN, y_up), ag(c_x, p, 4, X_UP, y_dn))

    def relay_y(p):
        if p % 2 == 0:
            landed(FROM_DN, p)
            send(ag(c_dn, p, 5, TWO, y_up))
        else:
            landed(FROM_UP, p)
            send(ag(c_up, p, 5, TWO, y_dn))

    def relay_two(p):
        landed(TWO, p)
        send(ag(c_two, p, 6, X_TWO, x_near))

    inputs[2].wait()
    inputs[3].wait()
    prepare(0, 8)
    relay_y(0)
    relay_x(0)
    relay_y(1)
    relay_y(2)
    relay_x(1)
    relay_y(3)
    prepare(8, 12)
    relay_x(2)
    prepare(12, 16)
    relay_x(3)
    prepare(16, 20)
    relay_two(0)
    relay_two(1)
    prepare(20, 24)
    relay_two(2)
    relay_two(3)
    prepare(24, 32)
    for p in range(PIECES):
        landed(FROM_UP if p % 2 == 0 else FROM_DN, p)
        landed(X_DN, p)
        landed(X_UP, p)
    for p in range(PIECES):
        landed(X_TWO, p)
    inputs[4].wait()
    inputs[5].wait()

    def term(s):
        right = jnp.concatenate([gat[ids_ref[k, s] % 16] for k in range(SLOTS)], axis=0)
        return jnp.dot(left[s], right, preferred_element_type=F32)

    def sib_copy(i):
        return pltpu.make_async_remote_copy(
            src_ref=sib_out.at[i], dst_ref=sib_in.at[i], send_sem=sib_send.at[i], recv_sem=sib_recv.at[i],
            device_id=sib, device_id_type=MESH,
        )

    def part(p):
        return pl.ds(p * PIECE, PIECE)

    def x_copy(d, p):
        return pltpu.make_async_remote_copy(
            src_ref=z_out.at[TASK[0, d], part(p)], dst_ref=x_in.at[XSLOT[d], part(p)],
            send_sem=x_send.at[XSLOT[d], p], recv_sem=x_recv.at[XSLOT[d], p],
            device_id=x_far, device_id_type=MESH,
        )

    def z_copy(w, d, p):
        up = d > 0 and (d < 4 or p % 2 == 0)
        then = TASK[w, d - 1 if up else -3 if d == 4 else d + 1]
        down_last = d == -1
        return pltpu.make_async_remote_copy(
            src_ref=z_out.at[TASK[w, d], part(p)],
            dst_ref=z_in2.at[w, part(p)] if down_last else z_in.at[then, part(p)],
            send_sem=z_send.at[TASK[w, d], p],
            recv_sem=z_recv2.at[w, p] if down_last else z_recv.at[then, p],
            device_id=z_up if up else z_dn, device_id_type=MESH,
        )

    def next_hop(w, d, p):
        if w == 0 and (p in X_FIRST or d == 0):
            return x_copy(d, p)
        return None if d == 0 else z_copy(w, d, p)

    waited = set()

    def finish(w, d, p):
        i = TASK[w, d]
        if i not in waited:
            waited.add(i)
            sib_copy(i).wait_recv()
        value = own[i, part(p)] + sib_in[i, part(p)].astype(F32)
        if w == 1 and (p in X_FIRST or d == 0):
            x_copy(d, p).wait_recv()
            value = value + x_in[XSLOT[d], part(p)].astype(F32)
        if w == 1 or p not in X_FIRST:
            from_dn = d in (0, 1, 2) or (d == 3 and p % 2 == 0)
            from_up = d in (-1, -2) or (d == -3 and p % 2 == 1)
            if from_dn:
                z_copy(w, d + 1, p).wait_recv()
            if from_up:
                z_copy(w, 4 if d == -3 else d - 1, p).wait_recv()
            if from_dn or from_up:
                value = value + z_in[i, part(p)].astype(F32)
            if d == 0:
                z_copy(w, -1, p).wait_recv()
                value = value + z_in2[w, part(p)].astype(F32)
        copy = next_hop(w, d, p)
        if copy is not None:
            z_out[i, part(p)] = value.astype(BF)
            copy.start()
            return
        mine = gat[2 * col + p // 2, pl.ds((p % 2) * PIECE, PIECE)].astype(F32)
        combined = (scal[part(p)] * (value + mine)).astype(BF)
        mixed = jnp.dot(combined, weight_ref[...], preferred_element_type=F32) + bias_ref[...]
        out_ref[part(p)] = jnp.maximum(mixed, 0.0).astype(BF)

    def follow(made):
        for piece in FOLLOW[made]:
            finish(*piece)

    def step(i, carry):
        w, d = pick(HALF, i), pick(DIST, i)
        target_x = w * xh + (1 - w) * (1 - xh)
        target_z = (z + d + NZ) % NZ
        sib_out[i] = term(at(target_x, target_z, 1 - core)).astype(BF)
        sib_copy(i).start()
        own[i] = term(at(target_x, target_z, core))

        for made in FOLLOW:
            if made < 16:
                pl.when(i == made - 1)(functools.partial(follow, made))
        return carry

    lax.fori_loop(0, 16, step, 0)
    follow(16)

    for copy in sends:
        copy.wait_send()
    for i, (w, d) in enumerate(zip(HALF, DIST)):
        sib_copy(i).wait_send()
        for p in range(PIECES):
            copy = next_hop(w, d, p)
            if copy is not None:
                copy.wait_send()


def local(features, degrees, blocks, block_ids, counts, weight, out_bias):
    vmem = pl.BlockSpec(memory_space=pltpu.VMEM)
    anywhere = pl.BlockSpec(memory_space=pl.ANY)
    full = (ROWS, FEAT)
    dma = pltpu.SemaphoreType.DMA
    return pl.pallas_call(
        kernel,
        out_shape=jax.ShapeDtypeStruct(full, BF),
        in_specs=[anywhere] * 7,
        out_specs=vmem,
        scratch_shapes=[
            pltpu.VMEM((1, ROWS), jnp.int32),
            pltpu.VMEM(full, BF),
            pltpu.SMEM((SLOTS, SEGS), jnp.int32),
            pltpu.SMEM((1, SEGS), jnp.int32),
            pltpu.VMEM((FEAT, FEAT), BF),
            pltpu.VMEM((1, FEAT), F32),
            pltpu.VMEM((16, BS, FEAT), BF),
            pltpu.VMEM((SEGS, SLOTS, BS, BS), BF),
            pltpu.VMEM((SEGS, ROWS, SLOTS * BS), BF),
            pltpu.VMEM((16,) + full, F32),
            pltpu.VMEM((16,) + full, BF),
            pltpu.VMEM((16,) + full, BF),
            pltpu.VMEM((16,) + full, BF),
            pltpu.VMEM((16,) + full, BF),
            pltpu.VMEM((2,) + full, BF),
            pltpu.VMEM((8,) + full, BF),
            pltpu.VMEM((ROWS, 1), F32),
            dma((6,)), dma((8,)), dma((7, PIECES)), dma((7, PIECES)), dma((16,)), dma((16,)),
            dma((16, PIECES)), dma((16, PIECES)), dma((2, PIECES)), dma((8, PIECES)), dma((8, PIECES)),
        ],
        compiler_params=pltpu.CompilerParams(
            collective_id=0, has_side_effects=True, vmem_limit_bytes=60 * 1024 * 1024
        ),
        cost_estimate=pl.CostEstimate(
            flops=2 * SEGS * ROWS * SLOTS * BS * FEAT, bytes_accessed=SEGS * SLOTS * BS * BS * 2, transcendentals=0
        ),
    )(degrees.reshape(1, ROWS), features, blocks, block_ids.T, counts.T, weight, out_bias.reshape(1, FEAT))


def solution(mesh):
    placed = (
        P(("row", "col"), None),
        P(("row", "col")),
        P("row", "col", None, None),
        P("row", "col"),
        P("row", "col"),
        P(),
        P(),
    )
    return jax.shard_map(
        local, mesh=mesh, in_specs=placed, out_specs=P(("row", "col"), None), check_vma=False
    )
```

```python
import functools

import jax
import jax.numpy as jnp
from jax import lax
from jax.experimental import pallas as pl
from jax.experimental.pallas import tpu as pltpu
from jax.sharding import PartitionSpec as P

MESH = pl.DeviceIdType.MESH
BF = jnp.bfloat16
F32 = jnp.float32
NZ = 8
NY = 4
SEGS = 32
SLOTS = 11
BS = 128
ROWS = 256
FEAT = 256
PIECES = 4
PIECE = ROWS // PIECES
X_FIRST = (0, 1)
HALF = [0, 1, 0, 0, 1, 1, 0, 0, 1, 1, 0, 0, 1, 1, 0, 1]
DIST = [4, 4, 3, -3, -3, 3, 2, -2, -2, 2, -1, 1, 1, -1, 0, 0]
TASK = {pair: i for i, pair in enumerate(zip(HALF, DIST))}
XSLOT = {d: i for i, d in enumerate((4, 3, -3, 2, -2, 1, -1, 0))}
FOLLOW = {
    3: [(0, 4, 1), (0, 4, 0), (0, 4, 3), (0, 4, 2)],
    4: [(1, 4, 3), (0, 3, 1), (0, 3, 0), (1, 4, 2), (0, 3, 3)],
    5: [(0, -3, 1), (0, -3, 0), (0, -3, 2)],
    6: [(1, 4, 1), (0, -3, 3), (0, 3, 2), (1, -3, 2), (1, 4, 0)],
    7: [(1, 3, 3), (1, 3, 2), (1, 3, 1), (1, -3, 3)],
    9: [(0, 2, 1), (0, 2, 0), (1, -3, 1), (1, -3, 0), (0, 2, 3), (0, -2, 1), (0, -2, 0), (0, 2, 2), (0, -2, 3),
        (1, 3, 0), (0, -2, 2)],
    10: [(1, -2, 2)],
    11: [(1, -2, 3)],
    12: [(1, 2, 3), (1, 2, 2), (1, 2, 1)],
    13: [(0, -1, 1), (0, -1, 0), (0, 1, 1), (0, 1, 0), (1, -2, 1), (0, 1, 3), (0, 1, 2), (1, -2, 0), (1, 2, 0),
         (0, -1, 3), (0, -1, 2)],
    15: [(1, 1, 3)],
    16: [(1, 1, 2), (1, -1, 3), (1, -1, 2), (1, -1, 1), (0, 0, 1), (0, 0, 0), (1, -1, 0), (1, 1, 1), (0, 0, 3),
         (1, 1, 0), (0, 0, 2), (1, 0, 1), (1, 0, 3), (1, 0, 0), (1, 0, 2)],
}


def pick(table, index):
    value = jnp.int32(table[0])
    for i in range(1, len(table)):
        value = jnp.where(index >= i, jnp.int32(table[i]), value)
    return value


def kernel(
    deg_hbm, feat_hbm, blocks_ref, ids_hbm, cnt_hbm, weight_hbm, bias_hbm, out_ref,
    deg_ref, feat_ref, ids_ref, cnt_ref, weight_ref, bias_ref,
    gat, stage, left, own, sib_out, sib_in, z_out, z_in, z_in2, x_in, scal,
    in_sem, stage_sem, ag_send, ag_recv, sib_send, sib_recv, z_send, z_recv, z_recv2, x_send, x_recv,
):
    row, col = lax.axis_index("row"), lax.axis_index("col")
    core = row % 2
    z = (row // 2) % NZ
    xh = row // (2 * NZ)
    y, xl = col // 2, col % 2

    def at(xh_, z_, core_):
        return xh_ * (2 * NZ) + z_ * 2 + core_

    z_up = (at(xh, (z + 1) % NZ, core), col)
    z_dn = (at(xh, (z + NZ - 1) % NZ, core), col)
    sib = (at(xh, z, 1 - core), col)
    x_far = (at(1 - xh, z, core), col)
    c_up = ((y + 1) % NY) * 2 + xl
    c_dn = ((y + NY - 1) % NY) * 2 + xl
    c_x = y * 2 + 1 - xl
    c_two = ((y + 2) % NY) * 2 + xl
    y_up, y_dn, x_near = (row, c_up), (row, c_dn), (row, c_x)

    barrier = pltpu.get_barrier_semaphore()
    for other in (z_up, z_dn, sib, x_far, y_up, y_dn, x_near):
        pl.semaphore_signal(barrier, inc=1, device_id=other, device_id_type=MESH)

    inputs = [
        pltpu.make_async_copy(src, dst, in_sem.at[i])
        for i, (src, dst) in enumerate((
            (deg_hbm, deg_ref), (feat_hbm, feat_ref), (ids_hbm, ids_ref), (cnt_hbm, cnt_ref),
            (weight_hbm, weight_ref), (bias_hbm, bias_ref),
        ))
    ]
    for copy in inputs:
        copy.start()
    loads = [
        pltpu.make_async_copy(
            blocks_ref.at[pl.ds(4 * i, 4)], stage.at[pl.ds(4 * i, 4)], stage_sem.at[i]
        )
        for i in range(8)
    ]
    for load in loads:
        load.start()
    inputs[0].wait()
    inputs[1].wait()

    rows = lax.broadcasted_iota(jnp.int32, (ROWS, ROWS), 0)
    cols = lax.broadcasted_iota(jnp.int32, (ROWS, ROWS), 1)
    degs = jnp.broadcast_to(deg_ref[...].astype(F32), (ROWS, ROWS))
    scaling = lax.rsqrt(jnp.sum(jnp.where(rows == cols, degs, 0.0), axis=1, keepdims=True))
    scal[...] = scaling
    scaled = (feat_ref[...].astype(F32) * scaling).astype(BF)
    gat[2 * col] = scaled[:BS]
    gat[2 * col + 1] = scaled[BS:]

    pl.semaphore_wait(barrier, 7)

    def piece_of(source, p):
        return gat.at[2 * source + p // 2, pl.ds((p % 2) * PIECE, PIECE)]

    def ag(source, p, send, recv, target):
        return pltpu.make_async_remote_copy(
            src_ref=piece_of(source, p), dst_ref=piece_of(source, p),
            send_sem=ag_send.at[send, p], recv_sem=ag_recv.at[recv, p],
            device_id=target, device_id_type=MESH,
        )

    FROM_DN, FROM_UP, FROM_X, TWO, X_DN, X_UP, X_TWO = range(7)
    source_of = {
        FROM_DN: c_dn, FROM_UP: c_up, FROM_X: c_x, TWO: c_two,
        X_DN: ((y + NY - 1) % NY) * 2 + 1 - xl, X_UP: ((y + 1) % NY) * 2 + 1 - xl, X_TWO: ((y + 2) % NY) * 2 + 1 - xl,
    }
    sends = []

    def send(*copies):
        for copy in copies:
            copy.start()
            sends.append(copy)

    def landed(kind, p):
        ag(source_of[kind], p, 0, kind, y_up).wait_recv()

    for a, b, c in zip((0, 2, 1, 3), (1, 3, 0, 2), (0, 1, 2, 3)):
        send(ag(col, a, 0, FROM_DN, y_up), ag(col, c, 2, FROM_X, x_near), ag(col, b, 1, FROM_UP, y_dn))

    def prepare(first, last):
        for i in range(first // 4, last // 4):
            loads[i].wait()

        def body(s, carry):
            live = cnt_ref[0, s]
            for k in range(SLOTS):
                q = ids_ref[k, s]
                block = stage[s, k]
                top = jnp.where((q < 16) & (k < live), 1.0, 0.0).astype(F32)
                low = jnp.where((q >= 16) & (k < live), 1.0, 0.0).astype(F32)
                left[s, :BS, k * BS:(k + 1) * BS] = block * jnp.full((BS, BS), top, F32).astype(BF)
                left[s, BS:, k * BS:(k + 1) * BS] = block * jnp.full((BS, BS), low, F32).astype(BF)
            return carry

        lax.fori_loop(first, last, body, 0)

    def relay_x(p):
        landed(FROM_X, p)
        send(ag(c_x, p, 3, X_DN, y_up), ag(c_x, p, 4, X_UP, y_dn))

    def relay_y(p):
        if p % 2 == 0:
            landed(FROM_DN, p)
            send(ag(c_dn, p, 5, TWO, y_up))
        else:
            landed(FROM_UP, p)
            send(ag(c_up, p, 5, TWO, y_dn))

    def relay_two(p):
        landed(TWO, p)
        send(ag(c_two, p, 6, X_TWO, x_near))

    inputs[2].wait()
    inputs[3].wait()
    prepare(0, 8)
    relay_y(0)
    relay_x(0)
    relay_y(1)
    relay_y(2)
    relay_x(1)
    relay_y(3)
    prepare(8, 12)
    relay_x(2)
    prepare(12, 16)
    relay_x(3)
    prepare(16, 20)
    relay_two(0)
    relay_two(1)
    prepare(20, 24)
    relay_two(2)
    relay_two(3)
    prepare(24, 32)
    for p in range(PIECES):
        landed(FROM_UP if p % 2 == 0 else FROM_DN, p)
        landed(X_DN, p)
        landed(X_UP, p)
    for p in range(PIECES):
        landed(X_TWO, p)
    inputs[4].wait()
    inputs[5].wait()

    def term(s):
        right = jnp.concatenate([gat[ids_ref[k, s] % 16] for k in range(SLOTS)], axis=0)
        return jnp.dot(left[s], right, preferred_element_type=F32)

    def sib_copy(i):
        return pltpu.make_async_remote_copy(
            src_ref=sib_out.at[i], dst_ref=sib_in.at[i], send_sem=sib_send.at[i], recv_sem=sib_recv.at[i],
            device_id=sib, device_id_type=MESH,
        )

    def part(p):
        return pl.ds(p * PIECE, PIECE)

    def x_copy(d, p):
        return pltpu.make_async_remote_copy(
            src_ref=z_out.at[TASK[0, d], part(p)], dst_ref=x_in.at[XSLOT[d], part(p)],
            send_sem=x_send.at[XSLOT[d], p], recv_sem=x_recv.at[XSLOT[d], p],
            device_id=x_far, device_id_type=MESH,
        )

    def z_copy(w, d, p):
        up = d > 0 and (d < 4 or p % 2 == 0)
        then = TASK[w, d - 1 if up else -3 if d == 4 else d + 1]
        down_last = d == -1
        return pltpu.make_async_remote_copy(
            src_ref=z_out.at[TASK[w, d], part(p)],
            dst_ref=z_in2.at[w, part(p)] if down_last else z_in.at[then, part(p)],
            send_sem=z_send.at[TASK[w, d], p],
            recv_sem=z_recv2.at[w, p] if down_last else z_recv.at[then, p],
            device_id=z_up if up else z_dn, device_id_type=MESH,
        )

    def next_hop(w, d, p):
        if w == 0 and (p in X_FIRST or d == 0):
            return x_copy(d, p)
        return None if d == 0 else z_copy(w, d, p)

    waited = set()

    def finish(w, d, p):
        i = TASK[w, d]
        if i not in waited:
            waited.add(i)
            sib_copy(i).wait_recv()
        value = own[i, part(p)] + sib_in[i, part(p)].astype(F32)
        if w == 1 and (p in X_FIRST or d == 0):
            x_copy(d, p).wait_recv()
            value = value + x_in[XSLOT[d], part(p)].astype(F32)
        if w == 1 or p not in X_FIRST:
            from_dn = d in (0, 1, 2) or (d == 3 and p % 2 == 0)
            from_up = d in (-1, -2) or (d == -3 and p % 2 == 1)
            if from_dn:
                z_copy(w, d + 1, p).wait_recv()
            if from_up:
                z_copy(w, 4 if d == -3 else d - 1, p).wait_recv()
            if from_dn or from_up:
                value = value + z_in[i, part(p)].astype(F32)
            if d == 0:
                z_copy(w, -1, p).wait_recv()
                value = value + z_in2[w, part(p)].astype(F32)
        copy = next_hop(w, d, p)
        if copy is not None:
            z_out[i, part(p)] = value.astype(BF)
            copy.start()
            return
        mine = gat[2 * col + p // 2, pl.ds((p % 2) * PIECE, PIECE)].astype(F32)
        combined = (scal[part(p)] * (value + mine)).astype(BF)
        mixed = jnp.dot(combined, weight_ref[...], preferred_element_type=F32) + bias_ref[...]
        out_ref[part(p)] = jnp.maximum(mixed, 0.0).astype(BF)

    def follow(made):
        for piece in FOLLOW[made]:
            finish(*piece)

    def step(i, carry):
        w, d = pick(HALF, i), pick(DIST, i)
        target_x = w * xh + (1 - w) * (1 - xh)
        target_z = (z + d + NZ) % NZ
        theirs = term(at(target_x, target_z, 1 - core))
        ours = term(at(target_x, target_z, core))
        sib_out[i] = theirs.astype(BF)
        own[i] = ours
        sib_copy(i).start()

        for made in FOLLOW:
            if made < 16:
                pl.when(i == made - 1)(functools.partial(follow, made))
        return carry

    lax.fori_loop(0, 16, step, 0)
    follow(16)

    for copy in sends:
        copy.wait_send()
    for i, (w, d) in enumerate(zip(HALF, DIST)):
        sib_copy(i).wait_send()
        for p in range(PIECES):
            copy = next_hop(w, d, p)
            if copy is not None:
                copy.wait_send()


def local(features, degrees, blocks, block_ids, counts, weight, out_bias):
    vmem = pl.BlockSpec(memory_space=pltpu.VMEM)
    anywhere = pl.BlockSpec(memory_space=pl.ANY)
    full = (ROWS, FEAT)
    dma = pltpu.SemaphoreType.DMA
    return pl.pallas_call(
        kernel,
        out_shape=jax.ShapeDtypeStruct(full, BF),
        in_specs=[anywhere] * 7,
        out_specs=vmem,
        scratch_shapes=[
            pltpu.VMEM((1, ROWS), jnp.int32),
            pltpu.VMEM(full, BF),
            pltpu.SMEM((SLOTS, SEGS), jnp.int32),
            pltpu.SMEM((1, SEGS), jnp.int32),
            pltpu.VMEM((FEAT, FEAT), BF),
            pltpu.VMEM((1, FEAT), F32),
            pltpu.VMEM((16, BS, FEAT), BF),
            pltpu.VMEM((SEGS, SLOTS, BS, BS), BF),
            pltpu.VMEM((SEGS, ROWS, SLOTS * BS), BF),
            pltpu.VMEM((16,) + full, F32),
            pltpu.VMEM((16,) + full, BF),
            pltpu.VMEM((16,) + full, BF),
            pltpu.VMEM((16,) + full, BF),
            pltpu.VMEM((16,) + full, BF),
            pltpu.VMEM((2,) + full, BF),
            pltpu.VMEM((8,) + full, BF),
            pltpu.VMEM((ROWS, 1), F32),
            dma((6,)), dma((8,)), dma((7, PIECES)), dma((7, PIECES)), dma((16,)), dma((16,)),
            dma((16, PIECES)), dma((16, PIECES)), dma((2, PIECES)), dma((8, PIECES)), dma((8, PIECES)),
        ],
        compiler_params=pltpu.CompilerParams(
            collective_id=0, has_side_effects=True, vmem_limit_bytes=60 * 1024 * 1024
        ),
        cost_estimate=pl.CostEstimate(
            flops=2 * SEGS * ROWS * SLOTS * BS * FEAT, bytes_accessed=SEGS * SLOTS * BS * BS * 2, transcendentals=0
        ),
    )(degrees.reshape(1, ROWS), features, blocks, block_ids.T, counts.T, weight, out_bias.reshape(1, FEAT))


def solution(mesh):
    placed = (
        P(("row", "col"), None),
        P(("row", "col")),
        P("row", "col", None, None),
        P("row", "col"),
        P("row", "col"),
        P(),
        P(),
    )
    return jax.shard_map(
        local, mesh=mesh, in_specs=placed, out_specs=P(("row", "col"), None), check_vma=False
    )
```

```python
import functools

import jax
import jax.numpy as jnp
from jax import lax
from jax.experimental import pallas as pl
from jax.experimental.pallas import tpu as pltpu
from jax.sharding import PartitionSpec as P

MESH = pl.DeviceIdType.MESH
BF = jnp.bfloat16
F32 = jnp.float32
NZ = 8
NY = 4
SEGS = 32
SLOTS = 11
BS = 128
ROWS = 256
FEAT = 256
PIECES = 4
PIECE = ROWS // PIECES
BY_X = (0,)
X_FIRST = (0, 1)
HALF = [0, 1, 0, 0, 1, 1, 0, 0, 1, 1, 0, 0, 1, 1, 0, 1]
DIST = [4, 4, 3, -3, -3, 3, 2, -2, -2, 2, -1, 1, 1, -1, 0, 0]
TASK = {pair: i for i, pair in enumerate(zip(HALF, DIST))}
XSLOT = {d: i for i, d in enumerate((4, 3, -3, 2, -2, 1, -1, 0))}
FOLLOW = {
    3: [(0, 4, 1), (0, 4, 0), (0, 4, 3), (0, 4, 2)],
    4: [(1, 4, 3), (0, 3, 1), (0, 3, 0), (1, 4, 2), (0, 3, 3)],
    5: [(0, -3, 1), (0, -3, 0), (0, -3, 2)],
    6: [(1, 4, 1), (0, -3, 3), (0, 3, 2), (1, -3, 2), (1, 4, 0)],
    7: [(1, 3, 3), (1, 3, 2), (1, 3, 1), (1, -3, 3)],
    9: [(0, 2, 1), (0, 2, 0), (1, -3, 1), (1, -3, 0), (0, 2, 3), (0, -2, 1), (0, -2, 0), (0, 2, 2), (0, -2, 3),
        (1, 3, 0), (0, -2, 2)],
    10: [(1, -2, 2)],
    11: [(1, -2, 3)],
    12: [(1, 2, 3), (1, 2, 2), (1, 2, 1)],
    13: [(0, -1, 1), (0, -1, 0), (0, 1, 1), (0, 1, 0), (1, -2, 1), (0, 1, 3), (0, 1, 2), (1, -2, 0), (1, 2, 0),
         (0, -1, 3), (0, -1, 2)],
    15: [(1, 1, 3)],
    16: [(1, 1, 2), (1, -1, 3), (1, -1, 2), (1, -1, 1), (0, 0, 1), (0, 0, 0), (1, -1, 0), (1, 1, 1), (0, 0, 3),
         (1, 1, 0), (0, 0, 2), (1, 0, 1), (1, 0, 3), (1, 0, 0), (1, 0, 2)],
}


def pick(table, index):
    value = jnp.int32(table[0])
    for i in range(1, len(table)):
        value = jnp.where(index >= i, jnp.int32(table[i]), value)
    return value


def kernel(
    deg_hbm, feat_hbm, blocks_ref, ids_hbm, cnt_hbm, weight_hbm, bias_hbm, out_ref,
    deg_ref, feat_ref, ids_ref, cnt_ref, weight_ref, bias_ref,
    gat, stage, left, own, sib_out, sib_in, z_out, z_in, z_in2, x_in, scal,
    in_sem, stage_sem, ag_send, ag_recv, sib_send, sib_recv, z_send, z_recv, z_recv2, x_send, x_recv,
):
    row, col = lax.axis_index("row"), lax.axis_index("col")
    core = row % 2
    z = (row // 2) % NZ
    xh = row // (2 * NZ)
    y, xl = col // 2, col % 2

    def at(xh_, z_, core_):
        return xh_ * (2 * NZ) + z_ * 2 + core_

    z_up = (at(xh, (z + 1) % NZ, core), col)
    z_dn = (at(xh, (z + NZ - 1) % NZ, core), col)
    sib = (at(xh, z, 1 - core), col)
    x_far = (at(1 - xh, z, core), col)
    c_up = ((y + 1) % NY) * 2 + xl
    c_dn = ((y + NY - 1) % NY) * 2 + xl
    c_x = y * 2 + 1 - xl
    c_two = ((y + 2) % NY) * 2 + xl
    y_up, y_dn, y_two, x_near = (row, c_up), (row, c_dn), (row, c_two), (row, c_x)

    barrier = pltpu.get_barrier_semaphore()
    for other in (z_up, z_dn, sib, x_far, y_up, y_dn, y_two, x_near):
        pl.semaphore_signal(barrier, inc=1, device_id=other, device_id_type=MESH)

    inputs = [
        pltpu.make_async_copy(src, dst, in_sem.at[i])
        for i, (src, dst) in enumerate((
            (deg_hbm, deg_ref), (feat_hbm, feat_ref), (ids_hbm, ids_ref), (cnt_hbm, cnt_ref),
            (weight_hbm, weight_ref), (bias_hbm, bias_ref),
        ))
    ]
    for copy in inputs:
        copy.start()
    loads = [
        pltpu.make_async_copy(
            blocks_ref.at[pl.ds(4 * i, 4)], stage.at[pl.ds(4 * i, 4)], stage_sem.at[i]
        )
        for i in range(8)
    ]
    for load in loads:
        load.start()
    inputs[0].wait()
    inputs[1].wait()

    rows = lax.broadcasted_iota(jnp.int32, (ROWS, ROWS), 0)
    cols = lax.broadcasted_iota(jnp.int32, (ROWS, ROWS), 1)
    degs = jnp.broadcast_to(deg_ref[...].astype(F32), (ROWS, ROWS))
    scaling = lax.rsqrt(jnp.sum(jnp.where(rows == cols, degs, 0.0), axis=1, keepdims=True))
    scal[...] = scaling
    scaled = (feat_ref[...].astype(F32) * scaling).astype(BF)
    gat[2 * col] = scaled[:BS]
    gat[2 * col + 1] = scaled[BS:]

    pl.semaphore_wait(barrier, 8)

    def piece_of(source, p):
        return gat.at[2 * source + p // 2, pl.ds((p % 2) * PIECE, PIECE)]

    def ag(source, p, send, recv, target):
        return pltpu.make_async_remote_copy(
            src_ref=piece_of(source, p), dst_ref=piece_of(source, p),
            send_sem=ag_send.at[send, p], recv_sem=ag_recv.at[recv, p],
            device_id=target, device_id_type=MESH,
        )

    FROM_DN, FROM_UP, FROM_X, TWO, X_DN, X_UP, X_TWO = range(7)
    source_of = {
        FROM_DN: c_dn, FROM_UP: c_up, FROM_X: c_x, TWO: c_two,
        X_DN: ((y + NY - 1) % NY) * 2 + 1 - xl, X_UP: ((y + 1) % NY) * 2 + 1 - xl, X_TWO: ((y + 2) % NY) * 2 + 1 - xl,
    }
    sends = []

    def send(*copies):
        for copy in copies:
            copy.start()
            sends.append(copy)

    def landed(kind, p):
        ag(source_of[kind], p, 0, kind, y_up).wait_recv()

    for p in range(PIECES):
        send(ag(col, p, 5, TWO, y_two), ag(col, p, 2, FROM_X, x_near))
    for p in range(PIECES):
        send(ag(col, p, 0, FROM_DN, y_up), ag(col, p, 1, FROM_UP, y_dn))

    def prepare(first, last):
        for i in range(first // 4, last // 4):
            loads[i].wait()

        def body(s, carry):
            live = cnt_ref[0, s]
            for k in range(SLOTS):
                q = ids_ref[k, s]
                block = stage[s, k]
                top = jnp.where((q < 16) & (k < live), 1.0, 0.0).astype(F32)
                low = jnp.where((q >= 16) & (k < live), 1.0, 0.0).astype(F32)
                left[s, :BS, k * BS:(k + 1) * BS] = block * jnp.full((BS, BS), top, F32).astype(BF)
                left[s, BS:, k * BS:(k + 1) * BS] = block * jnp.full((BS, BS), low, F32).astype(BF)
            return carry

        lax.fori_loop(first, last, body, 0)

    def relay_x(p):
        landed(FROM_X, p)
        if p not in BY_X:
            send(ag(c_x, p, 3, X_DN, y_up), ag(c_x, p, 4, X_UP, y_dn))

    def relay_two(p):
        landed(TWO, p)
        send(ag(c_two, p, 6, X_TWO, x_near))

    def relay_y(p):
        landed(FROM_DN, p)
        landed(FROM_UP, p)
        if p in BY_X:
            send(ag(c_dn, p, 3, X_DN, x_near), ag(c_up, p, 4, X_UP, x_near))

    inputs[2].wait()
    inputs[3].wait()
    prepare(0, 8)
    relay_x(0)
    relay_two(0)
    prepare(8, 12)
    relay_x(1)
    relay_two(1)
    prepare(12, 16)
    relay_x(2)
    relay_two(2)
    relay_x(3)
    relay_two(3)
    prepare(16, 24)
    for p in range(PIECES):
        relay_y(p)
    prepare(24, 32)
    for p in range(PIECES):
        landed(X_TWO, p)
        landed(X_DN, p)
        landed(X_UP, p)
    inputs[4].wait()
    inputs[5].wait()

    def term(s):
        right = jnp.concatenate([gat[ids_ref[k, s] % 16] for k in range(SLOTS)], axis=0)
        return jnp.dot(left[s], right, preferred_element_type=F32)

    def sib_copy(i):
        return pltpu.make_async_remote_copy(
            src_ref=sib_out.at[i], dst_ref=sib_in.at[i], send_sem=sib_send.at[i], recv_sem=sib_recv.at[i],
            device_id=sib, device_id_type=MESH,
        )

    def part(p):
        return pl.ds(p * PIECE, PIECE)

    def x_copy(d, p):
        return pltpu.make_async_remote_copy(
            src_ref=z_out.at[TASK[0, d], part(p)], dst_ref=x_in.at[XSLOT[d], part(p)],
            send_sem=x_send.at[XSLOT[d], p], recv_sem=x_recv.at[XSLOT[d], p],
            device_id=x_far, device_id_type=MESH,
        )

    def z_copy(w, d, p):
        up = d > 0 and (d < 4 or p % 2 == 0)
        then = TASK[w, d - 1 if up else -3 if d == 4 else d + 1]
        down_last = d == -1
        return pltpu.make_async_remote_copy(
            src_ref=z_out.at[TASK[w, d], part(p)],
            dst_ref=z_in2.at[w, part(p)] if down_last else z_in.at[then, part(p)],
            send_sem=z_send.at[TASK[w, d], p],
            recv_sem=z_recv2.at[w, p] if down_last else z_recv.at[then, p],
            device_id=z_up if up else z_dn, device_id_type=MESH,
        )

    def next_hop(w, d, p):
        if w == 0 and (p in X_FIRST or d == 0):
            return x_copy(d, p)
        return None if d == 0 else z_copy(w, d, p)

    waited = set()

    def finish(w, d, p):
        i = TASK[w, d]
        if i not in waited:
            waited.add(i)
            sib_copy(i).wait_recv()
        value = own[i, part(p)] + sib_in[i, part(p)].astype(F32)
        if w == 1 and (p in X_FIRST or d == 0):
            x_copy(d, p).wait_recv()
            value = value + x_in[XSLOT[d], part(p)].astype(F32)
        if w == 1 or p not in X_FIRST:
            from_dn = d in (0, 1, 2) or (d == 3 and p % 2 == 0)
            from_up = d in (-1, -2) or (d == -3 and p % 2 == 1)
            if from_dn:
                z_copy(w, d + 1, p).wait_recv()
            if from_up:
                z_copy(w, 4 if d == -3 else d - 1, p).wait_recv()
            if from_dn or from_up:
                value = value + z_in[i, part(p)].astype(F32)
            if d == 0:
                z_copy(w, -1, p).wait_recv()
                value = value + z_in2[w, part(p)].astype(F32)
        copy = next_hop(w, d, p)
        if copy is not None:
            z_out[i, part(p)] = value.astype(BF)
            copy.start()
            return
        mine = gat[2 * col + p // 2, pl.ds((p % 2) * PIECE, PIECE)].astype(F32)
        combined = (scal[part(p)] * (value + mine)).astype(BF)
        mixed = jnp.dot(combined, weight_ref[...], preferred_element_type=F32) + bias_ref[...]
        out_ref[part(p)] = jnp.maximum(mixed, 0.0).astype(BF)

    def follow(made):
        for piece in FOLLOW[made]:
            finish(*piece)

    def step(i, carry):
        w, d = pick(HALF, i), pick(DIST, i)
        target_x = w * xh + (1 - w) * (1 - xh)
        target_z = (z + d + NZ) % NZ
        theirs = term(at(target_x, target_z, 1 - core))
        ours = term(at(target_x, target_z, core))
        sib_out[i] = theirs.astype(BF)
        own[i] = ours
        sib_copy(i).start()

        for made in FOLLOW:
            if made < 16:
                pl.when(i == made - 1)(functools.partial(follow, made))
        return carry

    lax.fori_loop(0, 16, step, 0)
    follow(16)

    for copy in sends:
        copy.wait_send()
    for i, (w, d) in enumerate(zip(HALF, DIST)):
        sib_copy(i).wait_send()
        for p in range(PIECES):
            copy = next_hop(w, d, p)
            if copy is not None:
                copy.wait_send()


def local(features, degrees, blocks, block_ids, counts, weight, out_bias):
    vmem = pl.BlockSpec(memory_space=pltpu.VMEM)
    anywhere = pl.BlockSpec(memory_space=pl.ANY)
    full = (ROWS, FEAT)
    dma = pltpu.SemaphoreType.DMA
    return pl.pallas_call(
        kernel,
        out_shape=pltpu.VMEM(full, BF),
        in_specs=[anywhere] * 7,
        out_specs=vmem,
        scratch_shapes=[
            pltpu.VMEM((1, ROWS), jnp.int32),
            pltpu.VMEM(full, BF),
            pltpu.SMEM((SLOTS, SEGS), jnp.int32),
            pltpu.SMEM((1, SEGS), jnp.int32),
            pltpu.VMEM((FEAT, FEAT), BF),
            pltpu.VMEM((1, FEAT), F32),
            pltpu.VMEM((16, BS, FEAT), BF),
            pltpu.VMEM((SEGS, SLOTS, BS, BS), BF),
            pltpu.VMEM((SEGS, ROWS, SLOTS * BS), BF),
            pltpu.VMEM((16,) + full, F32),
            pltpu.VMEM((16,) + full, BF),
            pltpu.VMEM((16,) + full, BF),
            pltpu.VMEM((16,) + full, BF),
            pltpu.VMEM((16,) + full, BF),
            pltpu.VMEM((2,) + full, BF),
            pltpu.VMEM((8,) + full, BF),
            pltpu.VMEM((ROWS, 1), F32),
            dma((6,)), dma((8,)), dma((7, PIECES)), dma((7, PIECES)), dma((16,)), dma((16,)),
            dma((16, PIECES)), dma((16, PIECES)), dma((2, PIECES)), dma((8, PIECES)), dma((8, PIECES)),
        ],
        compiler_params=pltpu.CompilerParams(
            collective_id=0, has_side_effects=True, vmem_limit_bytes=60 * 1024 * 1024
        ),
        cost_estimate=pl.CostEstimate(
            flops=2 * SEGS * ROWS * SLOTS * BS * FEAT, bytes_accessed=SEGS * SLOTS * BS * BS * 2, transcendentals=0
        ),
    )(degrees.reshape(1, ROWS), features, blocks, block_ids.T, counts.T, weight, out_bias.reshape(1, FEAT))


def solution(mesh):
    placed = (
        P(("row", "col"), None),
        P(("row", "col")),
        P("row", "col", None, None),
        P("row", "col"),
        P("row", "col"),
        P(),
        P(),
    )
    return jax.shard_map(
        local, mesh=mesh, in_specs=placed, out_specs=P(("row", "col"), None), check_vma=False
    )
```

```python
import functools

import jax
import jax.numpy as jnp
from jax import lax
from jax.experimental import pallas as pl
from jax.experimental.pallas import tpu as pltpu
from jax.sharding import PartitionSpec as P

MESH = pl.DeviceIdType.MESH
BF = jnp.bfloat16
F32 = jnp.float32
NZ = 8
NY = 4
SEGS = 32
SLOTS = 11
BS = 128
ROWS = 256
FEAT = 256
PIECES = 4
PIECE = ROWS // PIECES
BY_X = (0,)
X_FIRST = (0, 1)
HALF = [0, 1, 0, 0, 0, 1, 1, 0, 1, 1, 0, 0, 0, 1, 1, 1]
DIST = [4, 4, -3, 3, -2, 3, -3, 2, 2, -2, -1, 1, 0, -1, 1, 0]
TASK = {pair: i for i, pair in enumerate(zip(HALF, DIST))}
XSLOT = {d: i for i, d in enumerate((4, 3, -3, 2, -2, 1, -1, 0))}
FOLLOW = {
    3: [(0, 4, 3), (0, 4, 2), (0, 4, 0), (0, 4, 1)],
    4: [(1, 4, 3), (1, 4, 2)],
    5: [(0, -3, 1), (0, -3, 0), (0, -3, 2)],
    6: [(0, 3, 0), (0, 3, 3), (0, 3, 1)],
    7: [(0, -3, 3), (1, 4, 0), (0, -2, 1), (0, -2, 0), (0, 3, 2), (1, 3, 3), (1, 4, 1)],
    8: [(1, 3, 2), (1, -3, 2), (1, -3, 3)],
    9: [(0, -2, 2), (1, -3, 0)],
    10: [(0, 2, 3), (0, 2, 0), (0, 2, 1), (0, -2, 3), (1, 3, 0), (1, 3, 1)],
    11: [(1, -3, 1), (0, 2, 2)],
    12: [(1, -2, 2), (1, 2, 3)],
    13: [(0, -1, 0), (1, -2, 3), (0, -1, 1), (1, 2, 2), (0, -1, 2), (0, 1, 3), (0, 1, 1), (0, 1, 0)],
    14: [(1, -2, 0), (1, 2, 0), (0, -1, 3), (0, 0, 1), (0, 0, 0), (1, 2, 1)],
    15: [(1, -2, 1), (0, 1, 2)],
    16: [(1, -1, 2), (1, -1, 3), (1, 1, 3), (1, 1, 2), (1, -1, 0), (1, 1, 0), (0, 0, 3), (1, 1, 1), (1, -1, 1),
        (0, 0, 2), (1, 0, 0), (1, 0, 3), (1, 0, 1), (1, 0, 2)],
}


def pick(table, index):
    value = jnp.int32(table[0])
    for i in range(1, len(table)):
        value = jnp.where(index >= i, jnp.int32(table[i]), value)
    return value


def kernel(
    deg_hbm, feat_hbm, blocks_ref, ids_hbm, cnt_hbm, weight_hbm, bias_hbm, out_ref,
    deg_ref, feat_ref, ids_ref, cnt_ref, weight_ref, bias_ref,
    gat, stage, left, own, sib_out, sib_in, z_out, z_in, z_in2, x_in, scal,
    in_sem, stage_sem, ag_send, ag_recv, sib_send, sib_recv, z_send, z_recv, z_recv2, x_send, x_recv,
):
    row, col = lax.axis_index("row"), lax.axis_index("col")
    core = row % 2
    z = (row // 2) % NZ
    xh = row // (2 * NZ)
    y, xl = col // 2, col % 2

    def at(xh_, z_, core_):
        return xh_ * (2 * NZ) + z_ * 2 + core_

    z_up = (at(xh, (z + 1) % NZ, core), col)
    z_dn = (at(xh, (z + NZ - 1) % NZ, core), col)
    sib = (at(xh, z, 1 - core), col)
    x_far = (at(1 - xh, z, core), col)
    c_up = ((y + 1) % NY) * 2 + xl
    c_dn = ((y + NY - 1) % NY) * 2 + xl
    c_x = y * 2 + 1 - xl
    c_two = ((y + 2) % NY) * 2 + xl
    y_up, y_dn, y_two, x_near = (row, c_up), (row, c_dn), (row, c_two), (row, c_x)

    barrier = pltpu.get_barrier_semaphore()
    for other in (z_up, z_dn, sib, x_far, y_up, y_dn, y_two, x_near):
        pl.semaphore_signal(barrier, inc=1, device_id=other, device_id_type=MESH)

    inputs = [
        pltpu.make_async_copy(src, dst, in_sem.at[i])
        for i, (src, dst) in enumerate((
            (deg_hbm, deg_ref), (feat_hbm, feat_ref), (ids_hbm, ids_ref), (cnt_hbm, cnt_ref),
            (weight_hbm, weight_ref), (bias_hbm, bias_ref),
        ))
    ]
    for copy in inputs:
        copy.start()
    loads = [
        pltpu.make_async_copy(
            blocks_ref.at[pl.ds(4 * i, 4)], stage.at[pl.ds(4 * i, 4)], stage_sem.at[i]
        )
        for i in range(8)
    ]
    for load in loads:
        load.start()
    inputs[0].wait()
    inputs[1].wait()

    rows = lax.broadcasted_iota(jnp.int32, (ROWS, ROWS), 0)
    cols = lax.broadcasted_iota(jnp.int32, (ROWS, ROWS), 1)
    degs = jnp.broadcast_to(deg_ref[...].astype(F32), (ROWS, ROWS))
    scaling = lax.rsqrt(jnp.sum(jnp.where(rows == cols, degs, 0.0), axis=1, keepdims=True))
    scal[...] = scaling
    scaled = (feat_ref[...].astype(F32) * scaling).astype(BF)
    gat[2 * col] = scaled[:BS]
    gat[2 * col + 1] = scaled[BS:]

    pl.semaphore_wait(barrier, 8)

    def piece_of(source, p):
        return gat.at[2 * source + p // 2, pl.ds((p % 2) * PIECE, PIECE)]

    def ag(source, p, send, recv, target):
        return pltpu.make_async_remote_copy(
            src_ref=piece_of(source, p), dst_ref=piece_of(source, p),
            send_sem=ag_send.at[send, p], recv_sem=ag_recv.at[recv, p],
            device_id=target, device_id_type=MESH,
        )

    FROM_DN, FROM_UP, FROM_X, TWO, X_DN, X_UP, X_TWO = range(7)
    source_of = {
        FROM_DN: c_dn, FROM_UP: c_up, FROM_X: c_x, TWO: c_two,
        X_DN: ((y + NY - 1) % NY) * 2 + 1 - xl, X_UP: ((y + 1) % NY) * 2 + 1 - xl, X_TWO: ((y + 2) % NY) * 2 + 1 - xl,
    }
    sends = []

    def send(*copies):
        for copy in copies:
            copy.start()
            sends.append(copy)

    def landed(kind, p):
        ag(source_of[kind], p, 0, kind, y_up).wait_recv()

    for p in range(PIECES):
        send(ag(col, p, 5, TWO, y_two), ag(col, p, 2, FROM_X, x_near))
    for p in range(PIECES):
        send(ag(col, p, 0, FROM_DN, y_up), ag(col, p, 1, FROM_UP, y_dn))

    def prepare(first, last):
        for i in range(first // 4, last // 4):
            loads[i].wait()

        def body(s, carry):
            live = cnt_ref[0, s]
            for k in range(SLOTS):
                q = ids_ref[k, s]
                block = stage[s, k]
                top = jnp.where((q < 16) & (k < live), 1.0, 0.0).astype(F32)
                low = jnp.where((q >= 16) & (k < live), 1.0, 0.0).astype(F32)
                left[s, :BS, k * BS:(k + 1) * BS] = block * jnp.full((BS, BS), top, F32).astype(BF)
                left[s, BS:, k * BS:(k + 1) * BS] = block * jnp.full((BS, BS), low, F32).astype(BF)
            return carry

        lax.fori_loop(first, last, body, 0)

    def relay_x(p):
        landed(FROM_X, p)
        if p not in BY_X:
            send(ag(c_x, p, 3, X_DN, y_up), ag(c_x, p, 4, X_UP, y_dn))

    def relay_two(p):
        landed(TWO, p)
        send(ag(c_two, p, 6, X_TWO, x_near))

    def relay_y(p):
        landed(FROM_DN, p)
        landed(FROM_UP, p)
        if p in BY_X:
            send(ag(c_dn, p, 3, X_DN, x_near), ag(c_up, p, 4, X_UP, x_near))

    inputs[2].wait()
    inputs[3].wait()
    prepare(0, 8)
    relay_x(0)
    relay_two(0)
    prepare(8, 12)
    relay_x(1)
    relay_two(1)
    prepare(12, 16)
    relay_x(2)
    relay_two(2)
    relay_x(3)
    relay_two(3)
    prepare(16, 24)
    for p in range(PIECES):
        relay_y(p)
    prepare(24, 32)
    for p in range(PIECES):
        landed(X_TWO, p)
        landed(X_DN, p)
        landed(X_UP, p)
    inputs[4].wait()
    inputs[5].wait()

    def term(s):
        right = jnp.concatenate([gat[ids_ref[k, s] % 16] for k in range(SLOTS)], axis=0)
        return jnp.dot(left[s], right, preferred_element_type=F32)

    def sib_copy(i):
        return pltpu.make_async_remote_copy(
            src_ref=sib_out.at[i], dst_ref=sib_in.at[i], send_sem=sib_send.at[i], recv_sem=sib_recv.at[i],
            device_id=sib, device_id_type=MESH,
        )

    def part(p):
        return pl.ds(p * PIECE, PIECE)

    def x_copy(d, p):
        return pltpu.make_async_remote_copy(
            src_ref=z_out.at[TASK[0, d], part(p)], dst_ref=x_in.at[XSLOT[d], part(p)],
            send_sem=x_send.at[XSLOT[d], p], recv_sem=x_recv.at[XSLOT[d], p],
            device_id=x_far, device_id_type=MESH,
        )

    def z_copy(w, d, p):
        up = d > 0 and (d < 4 or p % 2 == 0)
        then = TASK[w, d - 1 if up else -3 if d == 4 else d + 1]
        down_last = d == -1
        return pltpu.make_async_remote_copy(
            src_ref=z_out.at[TASK[w, d], part(p)],
            dst_ref=z_in2.at[w, part(p)] if down_last else z_in.at[then, part(p)],
            send_sem=z_send.at[TASK[w, d], p],
            recv_sem=z_recv2.at[w, p] if down_last else z_recv.at[then, p],
            device_id=z_up if up else z_dn, device_id_type=MESH,
        )

    def next_hop(w, d, p):
        if w == 0 and (p in X_FIRST or d == 0):
            return x_copy(d, p)
        return None if d == 0 else z_copy(w, d, p)

    waited = set()

    def finish(w, d, p):
        i = TASK[w, d]
        if i not in waited:
            waited.add(i)
            sib_copy(i).wait_recv()
        value = own[i, part(p)] + sib_in[i, part(p)].astype(F32)
        if w == 1 and (p in X_FIRST or d == 0):
            x_copy(d, p).wait_recv()
            value = value + x_in[XSLOT[d], part(p)].astype(F32)
        if w == 1 or p not in X_FIRST:
            from_dn = d in (0, 1, 2) or (d == 3 and p % 2 == 0)
            from_up = d in (-1, -2) or (d == -3 and p % 2 == 1)
            if from_dn:
                z_copy(w, d + 1, p).wait_recv()
            if from_up:
                z_copy(w, 4 if d == -3 else d - 1, p).wait_recv()
            if from_dn or from_up:
                value = value + z_in[i, part(p)].astype(F32)
            if d == 0:
                z_copy(w, -1, p).wait_recv()
                value = value + z_in2[w, part(p)].astype(F32)
        copy = next_hop(w, d, p)
        if copy is not None:
            z_out[i, part(p)] = value.astype(BF)
            copy.start()
            return
        mine = gat[2 * col + p // 2, pl.ds((p % 2) * PIECE, PIECE)].astype(F32)
        combined = (scal[part(p)] * (value + mine)).astype(BF)
        mixed = jnp.dot(combined, weight_ref[...], preferred_element_type=F32) + bias_ref[...]
        out_ref[part(p)] = jnp.maximum(mixed, 0.0).astype(BF)

    def follow(made):
        for piece in FOLLOW[made]:
            finish(*piece)

    def step(i, carry):
        w, d = pick(HALF, i), pick(DIST, i)
        target_x = w * xh + (1 - w) * (1 - xh)
        target_z = (z + d + NZ) % NZ
        theirs = term(at(target_x, target_z, 1 - core))
        ours = term(at(target_x, target_z, core))
        sib_out[i] = theirs.astype(BF)
        own[i] = ours
        sib_copy(i).start()

        for made in FOLLOW:
            if made < 16:
                pl.when(i == made - 1)(functools.partial(follow, made))
        return carry

    lax.fori_loop(0, 16, step, 0)
    follow(16)

    for copy in sends:
        copy.wait_send()
    for i, (w, d) in enumerate(zip(HALF, DIST)):
        sib_copy(i).wait_send()
        for p in range(PIECES):
            copy = next_hop(w, d, p)
            if copy is not None:
                copy.wait_send()


def local(features, degrees, blocks, block_ids, counts, weight, out_bias):
    vmem = pl.BlockSpec(memory_space=pltpu.VMEM)
    anywhere = pl.BlockSpec(memory_space=pl.ANY)
    full = (ROWS, FEAT)
    dma = pltpu.SemaphoreType.DMA
    return pl.pallas_call(
        kernel,
        out_shape=pltpu.VMEM(full, BF),
        in_specs=[anywhere] * 7,
        out_specs=vmem,
        scratch_shapes=[
            pltpu.VMEM((1, ROWS), jnp.int32),
            pltpu.VMEM(full, BF),
            pltpu.SMEM((SLOTS, SEGS), jnp.int32),
            pltpu.SMEM((1, SEGS), jnp.int32),
            pltpu.VMEM((FEAT, FEAT), BF),
            pltpu.VMEM((1, FEAT), F32),
            pltpu.VMEM((16, BS, FEAT), BF),
            pltpu.VMEM((SEGS, SLOTS, BS, BS), BF),
            pltpu.VMEM((SEGS, ROWS, SLOTS * BS), BF),
            pltpu.VMEM((16,) + full, F32),
            pltpu.VMEM((16,) + full, BF),
            pltpu.VMEM((16,) + full, BF),
            pltpu.VMEM((16,) + full, BF),
            pltpu.VMEM((16,) + full, BF),
            pltpu.VMEM((2,) + full, BF),
            pltpu.VMEM((8,) + full, BF),
            pltpu.VMEM((ROWS, 1), F32),
            dma((6,)), dma((8,)), dma((7, PIECES)), dma((7, PIECES)), dma((16,)), dma((16,)),
            dma((16, PIECES)), dma((16, PIECES)), dma((2, PIECES)), dma((8, PIECES)), dma((8, PIECES)),
        ],
        compiler_params=pltpu.CompilerParams(
            collective_id=0, has_side_effects=True, vmem_limit_bytes=60 * 1024 * 1024
        ),
        cost_estimate=pl.CostEstimate(
            flops=2 * SEGS * ROWS * SLOTS * BS * FEAT, bytes_accessed=SEGS * SLOTS * BS * BS * 2, transcendentals=0
        ),
    )(degrees.reshape(1, ROWS), features, blocks, block_ids.T, counts.T, weight, out_bias.reshape(1, FEAT))


def solution(mesh):
    placed = (
        P(("row", "col"), None),
        P(("row", "col")),
        P("row", "col", None, None),
        P("row", "col"),
        P("row", "col"),
        P(),
        P(),
    )
    return jax.shard_map(
        local, mesh=mesh, in_specs=placed, out_specs=P(("row", "col"), None), check_vma=False
    )
```

```python
import functools

import jax
import jax.numpy as jnp
from jax import lax
from jax.experimental import pallas as pl
from jax.experimental.pallas import tpu as pltpu
from jax.sharding import PartitionSpec as P

MESH = pl.DeviceIdType.MESH
BF = jnp.bfloat16
F32 = jnp.float32
NZ = 8
NY = 4
SEGS = 32
SLOTS = 11
BS = 128
ROWS = 256
FEAT = 256
PIECES = 4
PIECE = ROWS // PIECES
BY_X = (0,)
X_FIRST = (0, 1)
HALF = [0, 1, 0, 0, 0, 1, 1, 0, 1, 1, 0, 0, 0, 1, 1, 1]
DIST = [4, 4, -3, 3, -2, 3, -3, 2, 2, -2, -1, 1, 0, -1, 1, 0]
TASK = {pair: i for i, pair in enumerate(zip(HALF, DIST))}
XSLOT = {d: i for i, d in enumerate((4, 3, -3, 2, -2, 1, -1, 0))}
FOLLOW = {
    3: [(0, 4, 3), (0, 4, 2), (0, 4, 0), (0, 4, 1)],
    4: [(1, 4, 3), (1, 4, 2)],
    5: [(0, -3, 1), (0, -3, 0), (0, -3, 2)],
    6: [(0, 3, 0), (0, 3, 3), (0, 3, 1)],
    7: [(0, -3, 3), (1, 4, 0), (0, -2, 1), (0, -2, 0), (0, 3, 2), (1, 3, 3), (1, 4, 1)],
    8: [(1, 3, 2), (1, -3, 2), (1, -3, 3)],
    9: [(0, -2, 2), (1, -3, 0)],
    10: [(0, 2, 3), (0, 2, 0), (0, 2, 1), (0, -2, 3), (1, 3, 0), (1, 3, 1)],
    11: [(1, -3, 1), (0, 2, 2)],
    12: [(1, -2, 2), (1, 2, 3)],
    13: [(0, -1, 0), (1, -2, 3), (0, -1, 1), (1, 2, 2), (0, -1, 2), (0, 1, 3), (0, 1, 1), (0, 1, 0)],
    14: [(1, -2, 0), (1, 2, 0), (0, -1, 3), (0, 0, 1), (0, 0, 0), (1, 2, 1)],
    15: [(1, -2, 1), (0, 1, 2)],
    16: [(1, -1, 2), (1, -1, 3), (1, 1, 3), (1, 1, 2), (1, -1, 0), (1, 1, 0), (0, 0, 3), (1, 1, 1), (1, -1, 1),
        (0, 0, 2), (1, 0, 0), (1, 0, 3), (1, 0, 1), (1, 0, 2)],
}


def pick(table, index):
    value = jnp.int32(table[0])
    for i in range(1, len(table)):
        value = jnp.where(index >= i, jnp.int32(table[i]), value)
    return value


def kernel(
    deg_hbm, feat_hbm, blocks_ref, ids_hbm, cnt_hbm, weight_hbm, bias_hbm, out_ref,
    deg_ref, feat_ref, ids_ref, cnt_ref, weight_ref, bias_ref,
    gat, stage, left, own, sib_out, sib_in, z_out, z_in, z_in2, x_in, scal,
    in_sem, stage_sem, ag_send, ag_recv, sib_send, sib_recv, z_send, z_recv, z_recv2, x_send, x_recv,
):
    row, col = lax.axis_index("row"), lax.axis_index("col")
    core = row % 2
    z = (row // 2) % NZ
    xh = row // (2 * NZ)
    y, xl = col // 2, col % 2

    def at(xh_, z_, core_):
        return xh_ * (2 * NZ) + z_ * 2 + core_

    z_up = (at(xh, (z + 1) % NZ, core), col)
    z_dn = (at(xh, (z + NZ - 1) % NZ, core), col)
    sib = (at(xh, z, 1 - core), col)
    x_far = (at(1 - xh, z, core), col)
    c_up = ((y + 1) % NY) * 2 + xl
    c_dn = ((y + NY - 1) % NY) * 2 + xl
    c_x = y * 2 + 1 - xl
    c_two = ((y + 2) % NY) * 2 + xl
    y_up, y_dn, y_two, x_near = (row, c_up), (row, c_dn), (row, c_two), (row, c_x)

    barrier = pltpu.get_barrier_semaphore()
    for other in (z_up, z_dn, sib, x_far, y_up, y_dn, y_two, x_near):
        pl.semaphore_signal(barrier, inc=1, device_id=other, device_id_type=MESH)

    inputs = [
        pltpu.make_async_copy(src, dst, in_sem.at[i])
        for i, (src, dst) in enumerate((
            (deg_hbm, deg_ref), (feat_hbm, feat_ref), (ids_hbm, ids_ref), (cnt_hbm, cnt_ref),
            (weight_hbm, weight_ref), (bias_hbm, bias_ref),
        ))
    ]
    for copy in inputs:
        copy.start()
    loads = [
        pltpu.make_async_copy(
            blocks_ref.at[pl.ds(4 * i, 4)], stage.at[pl.ds(4 * i, 4)], stage_sem.at[i]
        )
        for i in range(8)
    ]
    for load in loads:
        load.start()
    inputs[0].wait()
    inputs[1].wait()

    rows = lax.broadcasted_iota(jnp.int32, (ROWS, ROWS), 0)
    cols = lax.broadcasted_iota(jnp.int32, (ROWS, ROWS), 1)
    degs = jnp.broadcast_to(deg_ref[...].astype(F32), (ROWS, ROWS))
    scaling = lax.rsqrt(jnp.sum(jnp.where(rows == cols, degs, 0.0), axis=1, keepdims=True))
    scal[...] = scaling
    scaled = (feat_ref[...].astype(F32) * scaling).astype(BF)
    gat[2 * col] = scaled[:BS]
    gat[2 * col + 1] = scaled[BS:]

    pl.semaphore_wait(barrier, 8)

    def piece_of(source, p):
        return gat.at[2 * source + p // 2, pl.ds((p % 2) * PIECE, PIECE)]

    def ag(source, p, send, recv, target):
        return pltpu.make_async_remote_copy(
            src_ref=piece_of(source, p), dst_ref=piece_of(source, p),
            send_sem=ag_send.at[send, p], recv_sem=ag_recv.at[recv, p],
            device_id=target, device_id_type=MESH,
        )

    FROM_DN, FROM_UP, FROM_X, TWO, X_DN, X_UP, X_TWO = range(7)
    source_of = {
        FROM_DN: c_dn, FROM_UP: c_up, FROM_X: c_x, TWO: c_two,
        X_DN: ((y + NY - 1) % NY) * 2 + 1 - xl, X_UP: ((y + 1) % NY) * 2 + 1 - xl, X_TWO: ((y + 2) % NY) * 2 + 1 - xl,
    }
    sends = []

    def send(*copies):
        for copy in copies:
            copy.start()
            sends.append(copy)

    def landed(kind, p):
        ag(source_of[kind], p, 0, kind, y_up).wait_recv()

    for p in range(PIECES):
        send(ag(col, p, 5, TWO, y_two), ag(col, p, 2, FROM_X, x_near))
    for p in range(PIECES):
        send(ag(col, p, 0, FROM_DN, y_up), ag(col, p, 1, FROM_UP, y_dn))

    def prepare(first, last):
        for i in range(first // 4, last // 4):
            loads[i].wait()

        def body(s, carry):
            live = cnt_ref[0, s]
            for k in range(SLOTS):
                q = ids_ref[k, s]
                block = stage[s, k]
                top = jnp.where((q < 16) & (k < live), 1.0, 0.0).astype(F32)
                low = jnp.where((q >= 16) & (k < live), 1.0, 0.0).astype(F32)
                left[s, :BS, k * BS:(k + 1) * BS] = block * jnp.full((BS, BS), top, F32).astype(BF)
                left[s, BS:, k * BS:(k + 1) * BS] = block * jnp.full((BS, BS), low, F32).astype(BF)
            return carry

        lax.fori_loop(first, last, body, 0)

    def relay_x(p):
        landed(FROM_X, p)
        if p not in BY_X:
            send(ag(c_x, p, 3, X_DN, y_up), ag(c_x, p, 4, X_UP, y_dn))

    def relay_two(p):
        landed(TWO, p)
        send(ag(c_two, p, 6, X_TWO, x_near))

    def relay_y(p):
        landed(FROM_DN, p)
        landed(FROM_UP, p)
        if p in BY_X:
            send(ag(c_dn, p, 3, X_DN, x_near), ag(c_up, p, 4, X_UP, x_near))

    inputs[2].wait()
    inputs[3].wait()
    prepare(0, 8)
    relay_x(0)
    relay_two(0)
    prepare(8, 12)
    relay_x(1)
    relay_two(1)
    prepare(12, 16)
    relay_x(2)
    relay_two(2)
    relay_x(3)
    relay_two(3)
    relay_y(0)
    prepare(16, 32)
    for p in range(1, PIECES):
        relay_y(p)
    for p in range(PIECES):
        landed(X_TWO, p)
        landed(X_DN, p)
        landed(X_UP, p)
    inputs[4].wait()
    inputs[5].wait()

    def term(s):
        right = jnp.concatenate([gat[ids_ref[k, s] % 16] for k in range(SLOTS)], axis=0)
        return jnp.dot(left[s], right, preferred_element_type=F32)

    def sib_copy(i):
        return pltpu.make_async_remote_copy(
            src_ref=sib_out.at[i], dst_ref=sib_in.at[i], send_sem=sib_send.at[i], recv_sem=sib_recv.at[i],
            device_id=sib, device_id_type=MESH,
        )

    def part(p):
        return pl.ds(p * PIECE, PIECE)

    def x_copy(d, p):
        return pltpu.make_async_remote_copy(
            src_ref=z_out.at[TASK[0, d], part(p)], dst_ref=x_in.at[XSLOT[d], part(p)],
            send_sem=x_send.at[XSLOT[d], p], recv_sem=x_recv.at[XSLOT[d], p],
            device_id=x_far, device_id_type=MESH,
        )

    def z_copy(w, d, p):
        up = d > 0 and (d < 4 or p % 2 == 0)
        then = TASK[w, d - 1 if up else -3 if d == 4 else d + 1]
        down_last = d == -1
        return pltpu.make_async_remote_copy(
            src_ref=z_out.at[TASK[w, d], part(p)],
            dst_ref=z_in2.at[w, part(p)] if down_last else z_in.at[then, part(p)],
            send_sem=z_send.at[TASK[w, d], p],
            recv_sem=z_recv2.at[w, p] if down_last else z_recv.at[then, p],
            device_id=z_up if up else z_dn, device_id_type=MESH,
        )

    def next_hop(w, d, p):
        if w == 0 and (p in X_FIRST or d == 0):
            return x_copy(d, p)
        return None if d == 0 else z_copy(w, d, p)

    waited = set()

    def finish(w, d, p):
        i = TASK[w, d]
        if i not in waited:
            waited.add(i)
            sib_copy(i).wait_recv()
        value = own[i, part(p)] + sib_in[i, part(p)].astype(F32)
        if w == 1 and (p in X_FIRST or d == 0):
            x_copy(d, p).wait_recv()
            value = value + x_in[XSLOT[d], part(p)].astype(F32)
        if w == 1 or p not in X_FIRST:
            from_dn = d in (0, 1, 2) or (d == 3 and p % 2 == 0)
            from_up = d in (-1, -2) or (d == -3 and p % 2 == 1)
            if from_dn:
                z_copy(w, d + 1, p).wait_recv()
            if from_up:
                z_copy(w, 4 if d == -3 else d - 1, p).wait_recv()
            if from_dn or from_up:
                value = value + z_in[i, part(p)].astype(F32)
            if d == 0:
                z_copy(w, -1, p).wait_recv()
                value = value + z_in2[w, part(p)].astype(F32)
        copy = next_hop(w, d, p)
        if copy is not None:
            z_out[i, part(p)] = value.astype(BF)
            copy.start()
            return
        mine = gat[2 * col + p // 2, pl.ds((p % 2) * PIECE, PIECE)].astype(F32)
        combined = (scal[part(p)] * (value + mine)).astype(BF)
        mixed = jnp.dot(combined, weight_ref[...], preferred_element_type=F32) + bias_ref[...]
        out_ref[part(p)] = jnp.maximum(mixed, 0.0).astype(BF)

    def follow(made):
        for piece in FOLLOW[made]:
            finish(*piece)

    def step(i, carry):
        w, d = pick(HALF, i), pick(DIST, i)
        target_x = w * xh + (1 - w) * (1 - xh)
        target_z = (z + d + NZ) % NZ
        theirs = term(at(target_x, target_z, 1 - core))
        ours = term(at(target_x, target_z, core))
        sib_out[i] = theirs.astype(BF)
        own[i] = ours
        sib_copy(i).start()

        for made in FOLLOW:
            if made < 16:
                pl.when(i == made - 1)(functools.partial(follow, made))
        return carry

    lax.fori_loop(0, 16, step, 0)
    follow(16)

    for copy in sends:
        copy.wait_send()
    for i, (w, d) in enumerate(zip(HALF, DIST)):
        sib_copy(i).wait_send()
        for p in range(PIECES):
            copy = next_hop(w, d, p)
            if copy is not None:
                copy.wait_send()


def local(features, degrees, blocks, block_ids, counts, weight, out_bias):
    vmem = pl.BlockSpec(memory_space=pltpu.VMEM)
    anywhere = pl.BlockSpec(memory_space=pl.ANY)
    full = (ROWS, FEAT)
    dma = pltpu.SemaphoreType.DMA
    return pl.pallas_call(
        kernel,
        out_shape=pltpu.VMEM(full, BF),
        in_specs=[anywhere] * 7,
        out_specs=vmem,
        scratch_shapes=[
            pltpu.VMEM((1, ROWS), jnp.int32),
            pltpu.VMEM(full, BF),
            pltpu.SMEM((SLOTS, SEGS), jnp.int32),
            pltpu.SMEM((1, SEGS), jnp.int32),
            pltpu.VMEM((FEAT, FEAT), BF),
            pltpu.VMEM((1, FEAT), F32),
            pltpu.VMEM((16, BS, FEAT), BF),
            pltpu.VMEM((SEGS, SLOTS, BS, BS), BF),
            pltpu.VMEM((SEGS, ROWS, SLOTS * BS), BF),
            pltpu.VMEM((16,) + full, F32),
            pltpu.VMEM((16,) + full, BF),
            pltpu.VMEM((16,) + full, BF),
            pltpu.VMEM((16,) + full, BF),
            pltpu.VMEM((16,) + full, BF),
            pltpu.VMEM((2,) + full, BF),
            pltpu.VMEM((8,) + full, BF),
            pltpu.VMEM((ROWS, 1), F32),
            dma((6,)), dma((8,)), dma((7, PIECES)), dma((7, PIECES)), dma((16,)), dma((16,)),
            dma((16, PIECES)), dma((16, PIECES)), dma((2, PIECES)), dma((8, PIECES)), dma((8, PIECES)),
        ],
        compiler_params=pltpu.CompilerParams(
            collective_id=0, has_side_effects=True, vmem_limit_bytes=60 * 1024 * 1024
        ),
        cost_estimate=pl.CostEstimate(
            flops=2 * SEGS * ROWS * SLOTS * BS * FEAT, bytes_accessed=SEGS * SLOTS * BS * BS * 2, transcendentals=0
        ),
    )(degrees.reshape(1, ROWS), features, blocks, block_ids.T, counts.T, weight, out_bias.reshape(1, FEAT))


def solution(mesh):
    placed = (
        P(("row", "col"), None),
        P(("row", "col")),
        P("row", "col", None, None),
        P("row", "col"),
        P("row", "col"),
        P(),
        P(),
    )
    return jax.shard_map(
        local, mesh=mesh, in_specs=placed, out_specs=P(("row", "col"), None), check_vma=False
    )
```

```python
import functools

import jax
import jax.numpy as jnp
from jax import lax
from jax.experimental import pallas as pl
from jax.experimental.pallas import tpu as pltpu
from jax.sharding import PartitionSpec as P

MESH = pl.DeviceIdType.MESH
BF = jnp.bfloat16
F32 = jnp.float32
NZ = 8
NY = 4
SEGS = 32
SLOTS = 11
BS = 128
ROWS = 256
FEAT = 256
PIECES = 4
PIECE = ROWS // PIECES
BY_X = (0,)
X_FIRST = (0, 1)
HALF = [0, 1, 0, 0, 1, 1, 0, 0, 1, 1, 0, 0, 1, 0, 1, 1]
DIST = [4, 4, 3, -3, -3, 3, -2, 2, -2, 2, -1, 1, 1, 0, -1, 0]
TASK = {pair: i for i, pair in enumerate(zip(HALF, DIST))}
XSLOT = {d: i for i, d in enumerate((4, 3, -3, 2, -2, 1, -1, 0))}
FOLLOW = {
    3: [(0, 4, 0), (0, 4, 2), (0, 4, 3), (0, 4, 1)],
    4: [(1, 4, 2), (1, 4, 3)],
    5: [(0, 3, 0), (0, 3, 1), (0, 3, 3)],
    6: [(0, -3, 2), (0, -3, 0), (0, -3, 1)],
    7: [(1, 4, 0), (0, -3, 3), (0, 3, 2), (1, 4, 1), (1, -3, 2), (1, 3, 3), (1, 3, 2), (1, -3, 3)],
    8: [(0, -2, 0), (0, -2, 1)],
    9: [(1, 3, 1), (0, -2, 2)],
    10: [(0, 2, 3), (0, 2, 1), (1, 3, 0), (0, -2, 3), (0, 2, 0), (1, -3, 0)],
    11: [(1, -3, 1), (0, 2, 2)],
    12: [(1, 2, 3), (1, -2, 2)],
    13: [(1, 2, 2), (1, -2, 3), (0, -1, 0), (0, -1, 2), (0, -1, 1), (1, 2, 1), (0, 1, 0), (0, 1, 1)],
    14: [(0, 1, 3), (0, -1, 3), (1, 2, 0), (1, -2, 0)],
    15: [(1, -2, 1), (0, 1, 2)],
    16: [(1, 1, 3), (0, 0, 1), (0, 0, 0), (1, 1, 2), (1, -1, 3), (1, -1, 2), (0, 0, 3), (1, 1, 1), (1, 1, 0),
        (1, -1, 0), (0, 0, 2), (1, -1, 1), (1, 0, 3), (1, 0, 0), (1, 0, 2), (1, 0, 1)],
}


def pick(table, index):
    value = jnp.int32(table[0])
    for i in range(1, len(table)):
        value = jnp.where(index >= i, jnp.int32(table[i]), value)
    return value


def kernel(
    deg_hbm, feat_hbm, blocks_ref, ids_hbm, cnt_hbm, weight_hbm, bias_hbm, out_ref,
    deg_ref, feat_ref, ids_ref, cnt_ref, weight_ref, bias_ref,
    gat, stage, left, own, sib_out, sib_in, z_out, z_in, z_in2, x_in, scal,
    in_sem, stage_sem, ag_send, ag_recv, sib_send, sib_recv, z_send, z_recv, z_recv2, x_send, x_recv,
):
    row, col = lax.axis_index("row"), lax.axis_index("col")
    core = row % 2
    z = (row // 2) % NZ
    xh = row // (2 * NZ)
    y, xl = col // 2, col % 2

    def at(xh_, z_, core_):
        return xh_ * (2 * NZ) + z_ * 2 + core_

    z_up = (at(xh, (z + 1) % NZ, core), col)
    z_dn = (at(xh, (z + NZ - 1) % NZ, core), col)
    sib = (at(xh, z, 1 - core), col)
    x_far = (at(1 - xh, z, core), col)
    c_up = ((y + 1) % NY) * 2 + xl
    c_dn = ((y + NY - 1) % NY) * 2 + xl
    c_x = y * 2 + 1 - xl
    c_two = ((y + 2) % NY) * 2 + xl
    y_up, y_dn, y_two, x_near = (row, c_up), (row, c_dn), (row, c_two), (row, c_x)

    barrier = pltpu.get_barrier_semaphore()
    for other in (z_up, z_dn, sib, x_far, y_up, y_dn, y_two, x_near):
        pl.semaphore_signal(barrier, inc=1, device_id=other, device_id_type=MESH)

    inputs = [
        pltpu.make_async_copy(src, dst, in_sem.at[i])
        for i, (src, dst) in enumerate((
            (deg_hbm, deg_ref), (feat_hbm, feat_ref), (ids_hbm, ids_ref), (cnt_hbm, cnt_ref),
            (weight_hbm, weight_ref), (bias_hbm, bias_ref),
        ))
    ]
    for copy in inputs:
        copy.start()
    loads = [
        pltpu.make_async_copy(
            blocks_ref.at[pl.ds(4 * i, 4)], stage.at[pl.ds(4 * i, 4)], stage_sem.at[i]
        )
        for i in range(8)
    ]
    for load in loads:
        load.start()
    inputs[0].wait()
    inputs[1].wait()

    rows = lax.broadcasted_iota(jnp.int32, (ROWS, ROWS), 0)
    cols = lax.broadcasted_iota(jnp.int32, (ROWS, ROWS), 1)
    degs = jnp.broadcast_to(deg_ref[...].astype(F32), (ROWS, ROWS))
    scaling = lax.rsqrt(jnp.sum(jnp.where(rows == cols, degs, 0.0), axis=1, keepdims=True))
    scal[...] = scaling
    scaled = (feat_ref[...].astype(F32) * scaling).astype(BF)
    gat[2 * col] = scaled[:BS]
    gat[2 * col + 1] = scaled[BS:]

    pl.semaphore_wait(barrier, 8)

    def piece_of(source, p):
        return gat.at[2 * source + p // 2, pl.ds((p % 2) * PIECE, PIECE)]

    def ag(source, p, send, recv, target):
        return pltpu.make_async_remote_copy(
            src_ref=piece_of(source, p), dst_ref=piece_of(source, p),
            send_sem=ag_send.at[send, p], recv_sem=ag_recv.at[recv, p],
            device_id=target, device_id_type=MESH,
        )

    FROM_DN, FROM_UP, FROM_X, TWO, X_DN, X_UP, X_TWO = range(7)
    source_of = {
        FROM_DN: c_dn, FROM_UP: c_up, FROM_X: c_x, TWO: c_two,
        X_DN: ((y + NY - 1) % NY) * 2 + 1 - xl, X_UP: ((y + 1) % NY) * 2 + 1 - xl, X_TWO: ((y + 2) % NY) * 2 + 1 - xl,
    }
    sends = []

    def send(*copies):
        for copy in copies:
            copy.start()
            sends.append(copy)

    def landed(kind, p):
        ag(source_of[kind], p, 0, kind, y_up).wait_recv()

    for p in range(PIECES):
        send(ag(col, p, 5, TWO, y_two), ag(col, p, 2, FROM_X, x_near))
    for p in range(PIECES):
        send(ag(col, p, 0, FROM_DN, y_up), ag(col, p, 1, FROM_UP, y_dn))

    def prepare(first, last):
        for i in range(first // 4, last // 4):
            loads[i].wait()

        def body(s, carry):
            live = cnt_ref[0, s]
            for k in range(SLOTS):
                q = ids_ref[k, s]
                block = stage[s, k]
                top = jnp.where((q < 16) & (k < live), 1.0, 0.0).astype(F32)
                low = jnp.where((q >= 16) & (k < live), 1.0, 0.0).astype(F32)
                left[s, :BS, k * BS:(k + 1) * BS] = block * jnp.full((BS, BS), top, F32).astype(BF)
                left[s, BS:, k * BS:(k + 1) * BS] = block * jnp.full((BS, BS), low, F32).astype(BF)
            return carry

        lax.fori_loop(first, last, body, 0)

    def relay_x(p):
        landed(FROM_X, p)
        if p not in BY_X:
            send(ag(c_x, p, 3, X_DN, y_up), ag(c_x, p, 4, X_UP, y_dn))

    def relay_two(p):
        landed(TWO, p)
        send(ag(c_two, p, 6, X_TWO, x_near))

    def relay_y(p):
        landed(FROM_DN, p)
        landed(FROM_UP, p)
        if p in BY_X:
            send(ag(c_dn, p, 3, X_DN, x_near), ag(c_up, p, 4, X_UP, x_near))

    inputs[2].wait()
    inputs[3].wait()
    prepare(0, 8)
    relay_x(0)
    relay_two(0)
    prepare(8, 12)
    relay_x(1)
    relay_two(1)
    prepare(12, 16)
    relay_x(2)
    relay_two(2)
    relay_x(3)
    relay_two(3)
    relay_y(0)
    prepare(16, 32)
    for p in range(1, PIECES):
        relay_y(p)
    for p in range(PIECES):
        landed(X_TWO, p)
        landed(X_DN, p)
        landed(X_UP, p)
    inputs[4].wait()
    inputs[5].wait()

    def term(s):
        right = jnp.concatenate([gat[ids_ref[k, s] % 16] for k in range(SLOTS)], axis=0)
        return jnp.dot(left[s], right, preferred_element_type=F32)

    def sib_copy(i):
        return pltpu.make_async_remote_copy(
            src_ref=sib_out.at[i], dst_ref=sib_in.at[i], send_sem=sib_send.at[i], recv_sem=sib_recv.at[i],
            device_id=sib, device_id_type=MESH,
        )

    def part(p):
        return pl.ds(p * PIECE, PIECE)

    def x_copy(d, p):
        return pltpu.make_async_remote_copy(
            src_ref=z_out.at[TASK[0, d], part(p)], dst_ref=x_in.at[XSLOT[d], part(p)],
            send_sem=x_send.at[XSLOT[d], p], recv_sem=x_recv.at[XSLOT[d], p],
            device_id=x_far, device_id_type=MESH,
        )

    def z_copy(w, d, p):
        up = d > 0 and (d < 4 or p % 2 == 0)
        then = TASK[w, d - 1 if up else -3 if d == 4 else d + 1]
        down_last = d == -1
        return pltpu.make_async_remote_copy(
            src_ref=z_out.at[TASK[w, d], part(p)],
            dst_ref=z_in2.at[w, part(p)] if down_last else z_in.at[then, part(p)],
            send_sem=z_send.at[TASK[w, d], p],
            recv_sem=z_recv2.at[w, p] if down_last else z_recv.at[then, p],
            device_id=z_up if up else z_dn, device_id_type=MESH,
        )

    def next_hop(w, d, p):
        if w == 0 and (p in X_FIRST or d == 0):
            return x_copy(d, p)
        return None if d == 0 else z_copy(w, d, p)

    waited = set()

    def finish(w, d, p):
        i = TASK[w, d]
        if i not in waited:
            waited.add(i)
            sib_copy(i).wait_recv()
        value = own[i, part(p)] + sib_in[i, part(p)].astype(F32)
        if w == 1 and (p in X_FIRST or d == 0):
            x_copy(d, p).wait_recv()
            value = value + x_in[XSLOT[d], part(p)].astype(F32)
        if w == 1 or p not in X_FIRST:
            from_dn = d in (0, 1, 2) or (d == 3 and p % 2 == 0)
            from_up = d in (-1, -2) or (d == -3 and p % 2 == 1)
            if from_dn:
                z_copy(w, d + 1, p).wait_recv()
            if from_up:
                z_copy(w, 4 if d == -3 else d - 1, p).wait_recv()
            if from_dn or from_up:
                value = value + z_in[i, part(p)].astype(F32)
            if d == 0:
                z_copy(w, -1, p).wait_recv()
                value = value + z_in2[w, part(p)].astype(F32)
        copy = next_hop(w, d, p)
        if copy is not None:
            z_out[i, part(p)] = value.astype(BF)
            copy.start()
            return
        mine = gat[2 * col + p // 2, pl.ds((p % 2) * PIECE, PIECE)].astype(F32)
        combined = (scal[part(p)] * (value + mine)).astype(BF)
        mixed = jnp.dot(combined, weight_ref[...], preferred_element_type=F32) + bias_ref[...]
        out_ref[part(p)] = jnp.maximum(mixed, 0.0).astype(BF)

    def follow(made):
        for piece in FOLLOW[made]:
            finish(*piece)

    def step(i, carry):
        w, d = pick(HALF, i), pick(DIST, i)
        target_x = w * xh + (1 - w) * (1 - xh)
        target_z = (z + d + NZ) % NZ
        theirs = term(at(target_x, target_z, 1 - core))
        ours = term(at(target_x, target_z, core))
        sib_out[i] = theirs.astype(BF)
        own[i] = ours
        sib_copy(i).start()

        for made in FOLLOW:
            if made < 16:
                pl.when(i == made - 1)(functools.partial(follow, made))
        return carry

    lax.fori_loop(0, 16, step, 0)
    follow(16)

    for copy in sends:
        copy.wait_send()
    for i, (w, d) in enumerate(zip(HALF, DIST)):
        sib_copy(i).wait_send()
        for p in range(PIECES):
            copy = next_hop(w, d, p)
            if copy is not None:
                copy.wait_send()


def local(features, degrees, blocks, block_ids, counts, weight, out_bias):
    vmem = pl.BlockSpec(memory_space=pltpu.VMEM)
    anywhere = pl.BlockSpec(memory_space=pl.ANY)
    full = (ROWS, FEAT)
    dma = pltpu.SemaphoreType.DMA
    return pl.pallas_call(
        kernel,
        out_shape=pltpu.VMEM(full, BF),
        in_specs=[anywhere] * 7,
        out_specs=vmem,
        scratch_shapes=[
            pltpu.VMEM((1, ROWS), jnp.int32),
            pltpu.VMEM(full, BF),
            pltpu.SMEM((SLOTS, SEGS), jnp.int32),
            pltpu.SMEM((1, SEGS), jnp.int32),
            pltpu.VMEM((FEAT, FEAT), BF),
            pltpu.VMEM((1, FEAT), F32),
            pltpu.VMEM((16, BS, FEAT), BF),
            pltpu.VMEM((SEGS, SLOTS, BS, BS), BF),
            pltpu.VMEM((SEGS, ROWS, SLOTS * BS), BF),
            pltpu.VMEM((16,) + full, F32),
            pltpu.VMEM((16,) + full, BF),
            pltpu.VMEM((16,) + full, BF),
            pltpu.VMEM((16,) + full, BF),
            pltpu.VMEM((16,) + full, BF),
            pltpu.VMEM((2,) + full, BF),
            pltpu.VMEM((8,) + full, BF),
            pltpu.VMEM((ROWS, 1), F32),
            dma((6,)), dma((8,)), dma((7, PIECES)), dma((7, PIECES)), dma((16,)), dma((16,)),
            dma((16, PIECES)), dma((16, PIECES)), dma((2, PIECES)), dma((8, PIECES)), dma((8, PIECES)),
        ],
        compiler_params=pltpu.CompilerParams(
            collective_id=0, has_side_effects=True, vmem_limit_bytes=60 * 1024 * 1024
        ),
        cost_estimate=pl.CostEstimate(
            flops=2 * SEGS * ROWS * SLOTS * BS * FEAT, bytes_accessed=SEGS * SLOTS * BS * BS * 2, transcendentals=0
        ),
    )(degrees.reshape(1, ROWS), features, blocks, block_ids.T, counts.T, weight, out_bias.reshape(1, FEAT))


def solution(mesh):
    placed = (
        P(("row", "col"), None),
        P(("row", "col")),
        P("row", "col", None, None),
        P("row", "col"),
        P("row", "col"),
        P(),
        P(),
    )
    return jax.shard_map(
        local, mesh=mesh, in_specs=placed, out_specs=P(("row", "col"), None), check_vma=False
    )
```
